512 devices in a mesh: req: 32 (over z, x), seq: 16 (over y, core).
Axes of the slice: x: 4, y: 8, z: 8, core: 2. Of those that a mesh axis runs over, the one named last changes fastest.
Arguments:
- transformer_tokens: bfloat16 [32, 96, 16, 64], P('req', None, 'seq'), may hold values from -6 to 6
- frames: int32 [32], replicated, may hold values from 1 to 96, as said below
- heights: int32 [32], replicated, may hold values from 4 to 8
- widths: int32 [32], replicated, may hold values from 4 to 8
- tile_decode_device: int32 [32, 16, 3], replicated, may hold values from -1 to 31, as said below
- tile_device_slot: int32 [32, 16, 3], replicated, may hold values from -1 to 1, as said below
- stem_conv_weight: bfloat16 [3, 3, 3, 16, 256], replicated, may hold values from -0.3125 to 0.3125
- stem_conv_bias: float32 [256], replicated, may hold values from -3 to 3
- upsample_first_weight: bfloat16 [3, 3, 3, 256, 256], replicated, may hold values from -0.078125 to 0.078125
- upsample_first_bias: float32 [256], replicated, may hold values from -3 to 3
- upsample_second_weight: bfloat16 [3, 3, 3, 256, 256], replicated, may hold values from -0.078125 to 0.078125
- upsample_second_bias: float32 [256], replicated, may hold values from -3 to 3
Outputs:
- decoded: bfloat16 [32, 16, 2, 2, 16, 16, 256], P('req', 'seq')
The draws below stay inside these ranges and needn't reach their ends.
Inputs may be any that keep to these rules, and one draw needn't show every extreme that they name: Request r has frames[r] latent frames, the rest of its 96 are padding. Of the two requests r and r + 16 exactly one has 96 frames; the other has at most 32. `tile_decode_device`: -1 exactly for tiles whose first frame is at or past the request's frame count; otherwise r or (r + 16) mod 32 for a tile of request r. `tile_device_slot`: -1 exactly where tile_decode_device is -1; no two tiles of a column share device and slot; in every frame column the request with 96 frames keeps exactly two of its three tiles on its own device and hands exactly one to its paired device, so that device is full in every column.
All inputs are finite; a program needn't handle non-finite values.
Results may differ from the reference program's by a relative error of at most 0.0043.
Values may be sent and summed in bfloat16 or wider, within the bound.
No kernel may reach another device: no remote copies, remote signals or barrier semaphores. Data moves between devices by JAX's collectives and lax.ppermute only.
A program may use at most 64 MiB of HBM per device.

```python
import jax
import jax.numpy as jnp
from jax import lax

LAT_C = 16
UP_C = 256
LAT_H = 8
LAT_W = 8
TF = 2
CAP = 2
TPD = 3
TOKEN_CHANNELS = 64
FRAME_TOKENS = 16
REQUEST_TOTAL = 32
SLABS = 16
FRAME_CAPACITY = 96


def plan(key):
    half = REQUEST_TOTAL // 2
    ids = jnp.arange(REQUEST_TOTAL, dtype=jnp.int32)
    pair = ids % half
    flip = jax.random.randint(jax.random.fold_in(key, 11), (half,), 0, 2).astype(jnp.int32)
    upper_half = (ids >= half).astype(jnp.int32)
    is_long = upper_half == flip[pair]
    spread = jax.random.randint(jax.random.fold_in(key, 12), (REQUEST_TOTAL,), 1, SLABS * TF + 1).astype(jnp.int32)
    spread = jnp.where(pair == 0, SLABS * TF, jnp.where(pair == 1, 1, spread))
    frame_counts = jnp.where(is_long, FRAME_CAPACITY, spread).astype(jnp.int32)
    partner = (ids + half) % REQUEST_TOTAL
    rows = jnp.arange(TPD, dtype=jnp.int32)
    columns = jnp.arange(SLABS, dtype=jnp.int32)
    tile_index = rows[None, None, :] * SLABS + columns[None, :, None]
    is_live = tile_index * TF < frame_counts[:, None, None]
    scores = jax.random.randint(jax.random.fold_in(key, 13), (REQUEST_TOTAL, SLABS, TPD), 0, 1 << 20).astype(jnp.int32) * TPD + rows[None, None, :]
    position = jnp.argsort(jnp.argsort(scores, axis=2, stable=True), axis=2, stable=True).astype(jnp.int32)
    short_slot = jax.random.randint(jax.random.fold_in(key, 14), (REQUEST_TOTAL, SLABS), 0, CAP).astype(jnp.int32)
    keep = position < CAP
    partner_slot = short_slot[partner]
    sent_index = position - CAP
    sent_slot = sent_index + (sent_index >= partner_slot[:, :, None]).astype(jnp.int32)
    long_device = jnp.where(keep, ids[:, None, None], partner[:, None, None])
    long_slot = jnp.where(keep, position, sent_slot)
    first_row = rows[None, None, :] == 0
    short_device = jnp.where(first_row, ids[:, None, None], -1)
    short_slot_all = jnp.where(first_row, short_slot[:, :, None], -1)
    device = jnp.where(is_long[:, None, None], long_device, short_device)
    slot_of = jnp.where(is_long[:, None, None], long_slot, short_slot_all)
    device = jnp.where(is_live, device, -1).astype(jnp.int32)
    slot_of = jnp.where(is_live, slot_of, -1).astype(jnp.int32)
    return (frame_counts, device, slot_of)


def draw_frames(key, part):
    shared = plan(key)
    return shared[0]


def draw_tile_decode_device(key, part):
    shared = plan(key)
    return shared[1]


def draw_tile_device_slot(key, part):
    shared = plan(key)
    return shared[2]


def draw_heights(key, part):
    key = jax.random.fold_in(key, 4)
    drawn = jax.random.randint(key, (REQUEST_TOTAL,), LAT_H // 2, LAT_H + 1)
    index = jnp.arange(REQUEST_TOTAL, dtype=jnp.int32)
    drawn = jnp.where(index == 0, LAT_H, drawn)
    return jnp.where(index == 1, LAT_H // 2, drawn).astype(jnp.int32)


def draw_widths(key, part):
    key = jax.random.fold_in(key, 5)
    drawn = jax.random.randint(key, (REQUEST_TOTAL,), LAT_W // 2, LAT_W + 1)
    index = jnp.arange(REQUEST_TOTAL, dtype=jnp.int32)
    drawn = jnp.where(index == 1, LAT_W, drawn)
    return jnp.where(index == 0, LAT_W // 2, drawn).astype(jnp.int32)


def steps_of(rng, shape, split, least, largest):
    level, own = 1.0, jax.random.fold_in(rng, 6)
    for dim, shards_of in split:
        draws = jnp.exp(jax.random.uniform(jax.random.fold_in(own, dim), (shards_of,), jnp.float32, least / len(split), largest / len(split)))
        level = level * jnp.repeat(draws, shape[dim] // shards_of).reshape([-1 if axis == dim else 1 for axis in range(len(shape))])
    return level


def gaussian(stream_key, shape, width, limit, cuts=(), kind=jnp.bfloat16):
    values = width * jax.random.normal(stream_key, shape, jnp.float32)
    if cuts:
        values = values * steps_of(stream_key, shape, cuts, -0.22, 0.18)
    return jnp.clip(values, -limit, limit).astype(kind)


def setup_inputs(seed: int = 0) -> dict:
    key_of = jax.random.split(jax.random.key(seed), 13)
    return {
        "transformer_tokens": gaussian(key_of[0], (REQUEST_TOTAL, FRAME_CAPACITY, FRAME_TOKENS, TOKEN_CHANNELS), 1.0, 6.0, ((0, 32), (2, 16))),
        "frames": draw_frames(jax.random.fold_in(key_of[12], 71), 0),
        "heights": draw_heights(jax.random.fold_in(key_of[12], 71), 0),
        "widths": draw_widths(jax.random.fold_in(key_of[12], 71), 0),
        "tile_decode_device": draw_tile_decode_device(jax.random.fold_in(key_of[12], 71), 0),
        "tile_device_slot": draw_tile_device_slot(jax.random.fold_in(key_of[12], 71), 0),
        "stem_conv_weight": gaussian(key_of[6], (3, 3, 3, LAT_C, UP_C), (27 * LAT_C) ** -0.5, 0.3125),
        "stem_conv_bias": gaussian(key_of[7], (UP_C,), 0.5, 3.0, (), jnp.float32),
        "upsample_first_weight": gaussian(key_of[8], (3, 3, 3, UP_C, UP_C), (27 * UP_C) ** -0.5, 0.078125),
        "upsample_first_bias": gaussian(key_of[9], (UP_C,), 0.5, 3.0, (), jnp.float32),
        "upsample_second_weight": gaussian(key_of[10], (3, 3, 3, UP_C, UP_C), (27 * UP_C) ** -0.5, 0.078125),
        "upsample_second_bias": gaussian(key_of[11], (UP_C,), 0.5, 3.0, (), jnp.float32),
    }


border_frames = 6


def unpatchify(tokens):
    lead = tokens.shape[:-2]
    half_rows = LAT_H // 2
    half_cols = LAT_W // 2
    shaped = tokens.reshape(lead + (half_rows, half_cols, LAT_C, 2, 2))
    count = len(lead)
    order = tuple(range(count)) + (count, count + 3, count + 1, count + 4, count + 2)
    return jnp.transpose(shaped, order).reshape(lead + (LAT_H, LAT_W, LAT_C))


def causal_conv(inputs, weight, biases):
    batch_size, frame_total, row_total, col_total, in_chans = inputs.shape
    out_frames = frame_total - 2
    padded = jnp.pad(inputs, ((0, 0), (0, 0), (1, 1), (1, 1), (0, 0)))
    kernel = weight.reshape(3, 3, 3 * in_chans, weight.shape[-1])
    summed = jnp.zeros((batch_size * out_frames * row_total * col_total, weight.shape[-1]), jnp.float32)
    for row_tap in range(3):
        for col_tap in range(3):
            window = padded[:, :, row_tap:row_tap + row_total, col_tap:col_tap + col_total, :]
            stacked = jnp.concatenate([window[:, time_tap:time_tap + out_frames] for time_tap in range(3)], axis=-1)
            summed = summed + jnp.dot(stacked.reshape(-1, 3 * in_chans), kernel[row_tap, col_tap], preferred_element_type=jnp.float32)
    return summed.reshape(batch_size, out_frames, row_total, col_total, -1) + biases


def region(frame_ok, scale, row_limit, col_limit, row_total, col_total):
    row_ok = jnp.arange(row_total, dtype=jnp.int32)[None, :] < (scale * row_limit)[:, None]
    col_ok = jnp.arange(col_total, dtype=jnp.int32)[None, :] < (scale * col_limit)[:, None]
    allowed = frame_ok[:, :, None, None] & row_ok[:, None, :, None] & col_ok[:, None, None, :]
    return allowed[..., None]


def stem(latent, window_start, frame_count, row_limit, col_limit, weight, biases):
    window = latent.shape[1]
    row_total = latent.shape[2]
    col_total = latent.shape[3]
    frame_at = window_start[:, None] + jnp.arange(window, dtype=jnp.int32)[None, :]
    started = frame_at >= 0
    visible = started & (frame_at < frame_count[:, None])
    inputs = jnp.where(region(visible, 1, row_limit, col_limit, row_total, col_total), latent, jnp.zeros((), latent.dtype))
    hidden = jax.nn.silu(causal_conv(inputs, weight, biases))
    return jnp.where(region(started[:, 2:], 1, row_limit, col_limit, row_total, col_total), hidden, 0.0).astype(jnp.bfloat16)


def upper(hidden_one, first_frame, frame_count, row_limit, col_limit, is_live, upsample_first_weight, upsample_first_bias, upsample_second_weight, upsample_second_bias):
    window = hidden_one.shape[1]
    row_total = hidden_one.shape[2]
    col_total = hidden_one.shape[3]
    frame_at = first_frame[:, None] + jnp.arange(window, dtype=jnp.int32)[None, :]
    started = frame_at >= 0
    finished = (frame_at < frame_count[:, None]) & is_live[:, None]
    hidden_two = jax.nn.silu(causal_conv(hidden_one, upsample_first_weight, upsample_first_bias))
    hidden_two = jnp.where(region(started[:, 2:], 1, row_limit, col_limit, row_total, col_total), hidden_two, 0.0).astype(jnp.bfloat16)
    upsampled = jnp.repeat(jnp.repeat(hidden_two, 2, axis=2), 2, axis=3)
    result = jax.nn.silu(causal_conv(upsampled, upsample_second_weight, upsample_second_bias))
    result = jnp.where(region(finished[:, 4:], 2, row_limit, col_limit, 2 * row_total, 2 * col_total), result, 0.0)
    return result.astype(jnp.bfloat16)


def reference(transformer_tokens, frames, heights, widths, tile_decode_device, tile_device_slot, stem_conv_weight, stem_conv_bias, upsample_first_weight, upsample_first_bias, upsample_second_weight, upsample_second_bias):
    tokens_padded_out = jnp.pad(transformer_tokens, ((0, 0), (border_frames, 0), (0, 0), (0, 0)))
    request_ids = jnp.arange(REQUEST_TOTAL, dtype=jnp.int32)
    row_ids = jnp.arange(TPD, dtype=jnp.int32)

    def one_slot(flat_index):
        device = flat_index // (SLABS * CAP)
        column = (flat_index // CAP) % SLABS
        slot_index = flat_index % CAP
        column_device = lax.dynamic_index_in_dim(tile_decode_device, column, 1, keepdims=False)
        column_slot = lax.dynamic_index_in_dim(tile_device_slot, column, 1, keepdims=False)
        matches = (column_device == device) & (column_slot == slot_index)
        is_live = jnp.any(matches)
        request = jnp.sum(jnp.where(matches, request_ids[:, None], 0)).astype(jnp.int32)
        row_index = jnp.sum(jnp.where(matches, row_ids[None, :], 0)).astype(jnp.int32)
        tile_index = row_index * SLABS + column
        zero = jnp.zeros((), jnp.int32)
        token_block = lax.dynamic_slice(tokens_padded_out, (request, (tile_index * TF).astype(jnp.int32), zero, zero), (1, TF + border_frames, FRAME_TOKENS, TOKEN_CHANNELS))
        latent = unpatchify(token_block)
        window_start = (tile_index * TF - border_frames).astype(jnp.int32)
        frame_count = frames[request][None]
        row_limit = heights[request][None]
        col_limit = widths[request][None]
        hidden_one = stem(latent, window_start[None], frame_count, row_limit, col_limit, stem_conv_weight, stem_conv_bias)
        result = upper(hidden_one, (window_start + 2)[None], frame_count, row_limit, col_limit, is_live[None], upsample_first_weight, upsample_first_bias, upsample_second_weight, upsample_second_bias)
        return result[0]

    result = lax.map(one_slot, jnp.arange(REQUEST_TOTAL * SLABS * CAP, dtype=jnp.int32))
    return result.reshape(REQUEST_TOTAL, SLABS, CAP, TF, 2 * LAT_H, 2 * LAT_W, UP_C)
```

```python
import functools

import jax
import jax.numpy as jnp
from jax import lax
from jax.experimental import pallas as pl
from jax.experimental.pallas import tpu as pltpu
from jax.sharding import PartitionSpec as P

F32 = jnp.float32
BF16 = jnp.bfloat16
I32 = jnp.int32
CH = 256
SEQ = 16
TILES = 3
VMEM_LIMIT = 56 * 1024 * 1024


def iota(shape, dim):
    return lax.broadcasted_iota(I32, shape, dim)


def one(mask):
    return jnp.where(mask, 1.0, 0.0).astype(BF16)


def prep_kernel(
    frames_ref,
    heights_ref,
    widths_ref,
    device_ref,
    slot_ref,
    stem_ref,
    second_ref,
    pick_ref,
    place_ref,
    limits_ref,
    lanes_ref,
    spread_ref,
    stem_out_ref,
    folded_ref,
):
    me = lax.axis_index("req")
    column = lax.axis_index("seq")
    half = frames_ref.shape[1] // 2
    partner = lax.rem(me + half, 2 * half)

    lane = iota((1, 32), 1)

    def entry(ref, who):
        return jnp.sum(jnp.where(lane == who, ref[...], 0), axis=1, keepdims=True)

    dest = iota((SEQ, 1), 0)
    tile_lane = iota((SEQ, 32), 1)

    def of_request(ref, tile, who):
        return jnp.sum(jnp.where(tile_lane == who, ref[tile], 0), axis=1, keepdims=True)

    codes = []
    lims = []
    tops = []
    for k in range(2):
        code = jnp.zeros((SEQ, 1), I32)
        live = jnp.zeros((SEQ, 1), I32)
        taken = jnp.zeros((SEQ, 1), I32)
        for i in range(TILES):
            start = 32 * i + 2 * dest - 6
            for who, offset in ((me, 0), (partner, 128)):
                hit = (of_request(device_ref, i, who) == me) & (
                    of_request(slot_ref, i, who) == k
                )
                code = code + jnp.where(hit, start + offset, 0)
                live = live + jnp.where(hit, 1, 0)
                if offset:
                    taken = taken + jnp.where(hit, 1, 0)
        lim = jnp.where(
            taken > 0,
            128 + entry(frames_ref, partner),
            jnp.where(live > 0, entry(frames_ref, me), 0),
        )
        code = jnp.where(live > 0, code, -64)
        codes.append(code)
        lims.append(lim)
        mine = dest == column

        def at_mine(v, mine=mine):
            return jnp.sum(jnp.where(mine, v, 0), axis=0, keepdims=True)

        my_taken = at_mine(taken) > 0
        my_live = at_mine(live) > 0
        tops.append(
            (
                jnp.where(my_taken, entry(heights_ref, partner), entry(heights_ref, me)),
                jnp.where(my_taken, entry(widths_ref, partner), entry(widths_ref, me)),
                at_mine(code) - jnp.where(my_taken, 128, 0),
                jnp.where(
                    my_live,
                    jnp.where(my_taken, entry(frames_ref, partner), entry(frames_ref, me)),
                    -64,
                ),
            )
        )

    source = iota((SEQ, 256), 1)
    for h in range(2):
        for k in range(2):
            for pair in range(4):
                row = (h * 8 + k * 4 + pair) * SEQ
                pick_ref[row : row + SEQ, :] = one(
                    (source == codes[k] + (2 * pair + h)) & (source < lims[k])
                )

    second_slot = iota((16, 128), 0) >= 8
    for n in range(4):
        limits_ref[n] = jnp.where(second_slot, tops[1][n], tops[0][n])

    row = iota((384, 128), 0)
    col = iota((384, 128), 1)
    tap = row >> 7
    y = (row >> 4) & 7
    which = (row >> 3) & 1
    x = (row & 7) + tap - 1
    tall = jnp.where(which == 1, tops[1][0], tops[0][0])
    wide = jnp.where(which == 1, tops[1][1], tops[0][1])
    wanted = ((y & 1) * 2 + (x & 1)) * 32 + which * 16 + (y >> 1) * 4 + (x >> 1)
    place_ref[...] = one((col == wanted) & (y < tall) & (x >= 0) & (x < wide))

    row = iota((512, 512), 0)
    col = iota((512, 512), 1)
    lanes_ref[...] = one(col == (row & 3) * 128 + (row >> 6) * 16 + ((row >> 2) & 15))

    row = iota((256, 768), 0)
    col = iota((256, 768), 1)
    step = (col >> 4) & 3
    spread_ref[...] = one(
        (row >> 7 == (col >> 6) & 1)
        & (step < 3)
        & ((row >> 4) & 7 == (col >> 7) + step)
        & (row & 15 == col & 15)
    )

    stem_out_ref[...] = jnp.zeros(stem_out_ref.shape, BF16)
    for dy in range(3):
        for dx in range(3):
            stem_out_ref[dy, dx * 64 : dx * 64 + 48, :] = stem_ref[dy * 3 + dx]

    def rows_of(u, w, t):
        return second_ref[u, w, t].astype(F32)

    def fold(t, carry):
        by_row = []
        for w in range(3):
            w0, w1, w2 = (rows_of(u, w, t) for u in range(3))
            by_row.append((w0, w1 + w2, w0 + w1, w2))
        for a in range(2):
            for ty in range(2):
                c0, c1, c2 = (by_row[w][2 * a + ty] for w in range(3))
                for b, tx, v in ((0, 0, c0), (0, 1, c1 + c2), (1, 0, c0 + c1), (1, 1, c2)):
                    folded_ref[((a * 2 + b) * 2 + ty) * 2 + tx, t] = v.astype(BF16)
        return carry

    lax.fori_loop(0, 3, fold, 0)


def pick_kernel(own_ref, other_ref, pick_ref, out_ref, rows_ref):
    gap = jnp.zeros((64, 32), BF16)
    both = jnp.concatenate([own_ref[...], gap, other_ref[...], gap], axis=1)
    picked = lax.dot_general(
        pick_ref[...], both, (((1,), (1,)), ((), ())), preferred_element_type=F32
    )
    joined = jnp.concatenate([picked[:128], picked[128:]], axis=1)
    for part in range(8):
        rows_ref[pl.ds(part, SEQ, stride=8), :] = joined[part * SEQ : (part + 1) * SEQ]
    out_ref[...] = rows_ref[...].astype(BF16).reshape(out_ref.shape)


def silu(v):
    halved = 0.5 * v
    return halved + halved * jnp.tanh(halved)


def store_taps(ref, frame, y, value):
    split = value.reshape(2, 8, CH)
    column = iota((2, 8, CH), 1)
    before = jnp.where(column == 0, 0.0, pltpu.roll(split, 1, 1))
    after = jnp.where(column == 7, 0.0, pltpu.roll(split, 7, 1))
    ref[0, frame, y + 1] = before.reshape(16, CH).astype(BF16)
    ref[1, frame, y + 1] = value.astype(BF16)
    ref[2, frame, y + 1] = after.reshape(16, CH).astype(BF16)


def main_kernel(
    tokens_ref,
    place_ref,
    limits_ref,
    lanes_ref,
    spread_ref,
    stem_ref,
    stem_bias_ref,
    first_hbm,
    first_bias_ref,
    folded_ref,
    second_bias_ref,
    out_ref,
    rows_ref,
    taps_ref,
    one_ref,
    two_ref,
    acc_ref,
    first_ref,
    mixed_ref,
    sems,
):
    copies = [
        pltpu.make_async_copy(first_hbm.at[u], first_ref.at[u], sems.at[u]) for u in range(3)
    ]
    for copy in copies:
        copy.start()

    rows_ref[...] = tokens_ref[...].reshape(128, 128).astype(F32)
    window = jnp.concatenate(
        [
            jnp.concatenate(
                [rows_ref[pl.ds(k * 4 + pair, SEQ, stride=8), :] for pair in range(4)], axis=1
            )
            for k in range(2)
        ],
        axis=0,
    ).astype(BF16)
    parity = jnp.dot(window, lanes_ref[...], preferred_element_type=F32).astype(BF16)
    stacked = jnp.concatenate([parity[:, n * 128 : (n + 1) * 128] for n in range(4)], axis=0)
    placed = jnp.dot(place_ref[...], stacked, preferred_element_type=F32).astype(BF16)
    near = jnp.dot(
        jnp.concatenate([placed[:128], placed[128:256]], axis=1),
        spread_ref[...],
        preferred_element_type=F32,
    ).astype(BF16)
    far = jnp.dot(
        placed[256:], spread_ref[:128], preferred_element_type=F32
    ).astype(BF16)
    zero_row = jnp.zeros((16, CH), BF16)
    for g in range(6):
        lanes = slice(g * 128, (g + 1) * 128)
        taps_ref[g, 0] = zero_row
        taps_ref[g, 1:9, :, :128] = near[:, lanes].reshape(8, 16, 128)
        taps_ref[g, 1:9, :, 128:] = far[:, lanes].reshape(8, 16, 128)
        taps_ref[g, 9] = zero_row
        for dx in range(3):
            one_ref[dx, g, 0] = zero_row
            one_ref[dx, g, 9] = zero_row
    for g in range(4):
        for dx in range(3):
            two_ref[dx, g, 0] = zero_row
            two_ref[dx, g, 9] = zero_row

    tall = limits_ref[0]
    wide = limits_ref[1]
    start = limits_ref[2]
    count = limits_ref[3]
    tall = jnp.concatenate([tall, tall], axis=1)
    wide = jnp.concatenate([wide, wide], axis=1)
    start = jnp.concatenate([start, start], axis=1)
    count = jnp.concatenate([count, count], axis=1)
    column = iota((16, CH), 0) & 7
    inside = column < wide

    def finish(frame, offset, y, total, bias, ref):
        value = silu(total + bias)
        keep = inside & (tall > y) & (start + offset + frame >= 0)
        store_taps(ref, frame, y, jnp.where(keep, value, 0.0))

    stem_bias = stem_bias_ref[...]
    hidden = jnp.dot(
        taps_ref[:, 0:8].reshape(768, CH), stem_ref[0], preferred_element_type=F32
    )
    for dy in range(1, 3):
        hidden = hidden + jnp.dot(
            taps_ref[:, dy : dy + 8].reshape(768, CH), stem_ref[dy], preferred_element_type=F32
        )
    hidden = hidden.reshape(6, 8, 16, CH)
    for g in range(6):
        for y in range(8):
            finish(g, 2, y, hidden[g, y], stem_bias, one_ref)

    first_bias = first_bias_ref[...]
    total = None
    for dy in range(3):
        copies[dy].wait()
        for dx in range(3):
            for dt in range(3):
                part = jnp.dot(
                    one_ref[dx, dt : dt + 4, dy : dy + 8].reshape(512, CH),
                    first_ref[dy, dx, dt],
                    preferred_element_type=F32,
                )
                total = part if total is None else total + part
    total = total.reshape(4, 8, 16, CH)
    for g in range(4):
        for y in range(8):
            finish(g, 4, y, total[g, y], first_bias, two_ref)

    second_bias = second_bias_ref[...]
    for a in range(2):
        for b in range(2):
            total = None
            for ty in range(2):
                for tx in range(2):
                    for dt in range(3):
                        part = jnp.dot(
                            two_ref[b + tx, dt : dt + 2, a + ty : a + ty + 8].reshape(256, CH),
                            folded_ref[((a * 2 + b) * 2 + ty) * 2 + tx, dt],
                            preferred_element_type=F32,
                        )
                        total = part if total is None else total + part
            total = total.reshape(2, 8, 16, CH)
            for f in range(2):
                for y in range(8):
                    value = silu(total[f, y] + second_bias)
                    keep = inside & (tall > y) & (start + 6 + f < count)
                    value = jnp.where(keep, value, 0.0)
                    for k in range(2):
                        row = ((k * 2 + f) * 16 + 2 * y + a) * 16 + b
                        for side in range(2):
                            mixed_ref[side, pl.ds(row, 8, stride=2), :] = value[
                                k * 8 : k * 8 + 8, side * 128 : side * 128 + 128
                            ]
    for side in range(2):
        out_ref[:, side * 128 : side * 128 + 128] = mixed_ref[side].astype(BF16)


def vmem_spec():
    return pl.BlockSpec(memory_space=pltpu.VMEM)


def body(
    transformer_tokens,
    frames,
    heights,
    widths,
    tile_decode_device,
    tile_device_slot,
    stem_conv_weight,
    stem_conv_bias,
    upsample_first_weight,
    upsample_first_bias,
    upsample_second_weight,
    upsample_second_bias,
):
    requests = lax.axis_size("req")
    half = requests // 2
    own = jnp.transpose(transformer_tokens[0, :, 0, :])
    other = lax.ppermute(own, "req", [(i, (i + half) % requests) for i in range(requests)])
    shape = jax.ShapeDtypeStruct
    pick, place, limits, lanes, spread, stem, folded = pl.pallas_call(
        prep_kernel,
        out_shape=(
            shape((256, 256), BF16),
            shape((384, 128), BF16),
            shape((4, 16, 128), I32),
            shape((512, 512), BF16),
            shape((256, 768), BF16),
            shape((3, 256, CH), BF16),
            shape((16, 3, CH, CH), BF16),
        ),
        in_specs=[vmem_spec()] * 7,
        out_specs=(vmem_spec(),) * 7,
        compiler_params=pltpu.CompilerParams(vmem_limit_bytes=VMEM_LIMIT),
    )(
        frames[None],
        heights[None],
        widths[None],
        jnp.transpose(tile_decode_device, (2, 1, 0)),
        jnp.transpose(tile_device_slot, (2, 1, 0)),
        stem_conv_weight.reshape(9, 48, CH),
        upsample_second_weight,
    )
    sent = pl.pallas_call(
        pick_kernel,
        out_shape=shape((SEQ, 8, 128), BF16),
        in_specs=[vmem_spec()] * 3,
        out_specs=vmem_spec(),
        scratch_shapes=[pltpu.VMEM((128, 128), F32)],
    )(own, other, pick)
    tokens = lax.all_to_all(sent, "seq", 0, 0, tiled=True)
    decoded = pl.pallas_call(
        main_kernel,
        out_shape=shape((1024, CH), BF16),
        in_specs=[vmem_spec()] * 7
        + [pl.BlockSpec(memory_space=pl.ANY)]
        + [vmem_spec()] * 3,
        out_specs=vmem_spec(),
        scratch_shapes=[
            pltpu.VMEM((128, 128), F32),
            pltpu.VMEM((6, 10, 16, CH), BF16),
            pltpu.VMEM((3, 6, 10, 16, CH), BF16),
            pltpu.VMEM((3, 4, 10, 16, CH), BF16),
            pltpu.VMEM((512, CH), F32),
            pltpu.VMEM((3, 3, 3, CH, CH), BF16),
            pltpu.VMEM((2, 1024, 128), F32),
            pltpu.SemaphoreType.DMA((3,)),
        ],
        compiler_params=pltpu.CompilerParams(vmem_limit_bytes=VMEM_LIMIT),
    )(
        tokens,
        place,
        limits,
        lanes,
        spread,
        stem,
        stem_conv_bias[None],
        upsample_first_weight,
        upsample_first_bias[None],
        folded,
        upsample_second_bias[None],
    )
    return decoded.reshape(1, 1, 2, 2, 16, 16, CH)


def solution(mesh):
    placed = (P("req", None, "seq", None), P(), P(), P(), P(), P(), P(), P(), P(), P(), P(), P())
    return jax.shard_map(
        body,
        mesh=mesh,
        in_specs=placed,
        out_specs=P("req", "seq", None, None, None, None, None),
        check_vma=False,
    )
```

```python
import functools

import jax
import jax.numpy as jnp
from jax import lax
from jax.experimental import pallas as pl
from jax.experimental.pallas import tpu as pltpu
from jax.sharding import PartitionSpec as P

F32 = jnp.float32
BF16 = jnp.bfloat16
I32 = jnp.int32
CH = 256
SEQ = 16
TILES = 3
VMEM_LIMIT = 52 * 1024 * 1024


def iota(shape, dim):
    return lax.broadcasted_iota(I32, shape, dim)


def one(mask):
    return jnp.where(mask, 1.0, 0.0).astype(BF16)


def plan_kernel(
    frames_ref,
    heights_ref,
    widths_ref,
    device_ref,
    slot_ref,
    pick_ref,
    place_ref,
    limits_ref,
):
    me = lax.axis_index("req")
    column = lax.axis_index("seq")
    half = frames_ref.shape[1] // 2
    partner = lax.rem(me + half, 2 * half)

    lane = iota((1, 32), 1)

    def entry(ref, who):
        return jnp.sum(jnp.where(lane == who, ref[...], 0), axis=1, keepdims=True)

    dest = iota((SEQ, 1), 0)
    tile_lane = iota((SEQ, 32), 1)

    def of_request(ref, tile, who):
        return jnp.sum(jnp.where(tile_lane == who, ref[tile], 0), axis=1, keepdims=True)

    codes = []
    lims = []
    tops = []
    for k in range(2):
        code = jnp.zeros((SEQ, 1), I32)
        live = jnp.zeros((SEQ, 1), I32)
        taken = jnp.zeros((SEQ, 1), I32)
        for i in range(TILES):
            start = 32 * i + 2 * dest - 6
            for who, offset in ((me, 0), (partner, 128)):
                hit = (of_request(device_ref, i, who) == me) & (
                    of_request(slot_ref, i, who) == k
                )
                code = code + jnp.where(hit, start + offset, 0)
                live = live + jnp.where(hit, 1, 0)
                if offset:
                    taken = taken + jnp.where(hit, 1, 0)
        lim = jnp.where(
            taken > 0,
            128 + entry(frames_ref, partner),
            jnp.where(live > 0, entry(frames_ref, me), 0),
        )
        code = jnp.where(live > 0, code, -64)
        codes.append(code)
        lims.append(lim)
        mine = dest == column

        def at_mine(v, mine=mine):
            return jnp.sum(jnp.where(mine, v, 0), axis=0, keepdims=True)

        my_taken = at_mine(taken) > 0
        my_live = at_mine(live) > 0
        tops.append(
            (
                jnp.where(my_taken, entry(heights_ref, partner), entry(heights_ref, me)),
                jnp.where(my_taken, entry(widths_ref, partner), entry(widths_ref, me)),
                at_mine(code) - jnp.where(my_taken, 128, 0),
                jnp.where(
                    my_live,
                    jnp.where(my_taken, entry(frames_ref, partner), entry(frames_ref, me)),
                    -64,
                ),
            )
        )

    source = iota((SEQ, 256), 1)
    for h in range(2):
        for k in range(2):
            for pair in range(4):
                row = (h * 8 + k * 4 + pair) * SEQ
                pick_ref[row : row + SEQ, :] = one(
                    (source == codes[k] + (2 * pair + h)) & (source < lims[k])
                )

    second_slot = iota((16, 128), 0) >= 8
    for n in range(4):
        limits_ref[n] = jnp.where(second_slot, tops[1][n], tops[0][n])

    row = iota((384, 128), 0)
    col = iota((384, 128), 1)
    tap = row >> 7
    y = (row >> 4) & 7
    which = (row >> 3) & 1
    x = (row & 7) + tap - 1
    tall = jnp.where(which == 1, tops[1][0], tops[0][0])
    wide = jnp.where(which == 1, tops[1][1], tops[0][1])
    wanted = ((y & 1) * 2 + (x & 1)) * 32 + which * 16 + (y >> 1) * 4 + (x >> 1)
    place_ref[...] = one((col == wanted) & (y < tall) & (x >= 0) & (x < wide))


def fold_kernel(
    sent_hbm,
    stem_ref,
    second_hbm,
    lanes_ref,
    spread_ref,
    stem_out_ref,
    folded_hbm,
    second_ref,
    folded_ref,
    in_sems,
    out_sems,
):
    ins = [
        pltpu.make_async_copy(second_hbm.at[:, :, t], second_ref.at[t], in_sems.at[t])
        for t in range(3)
    ]
    outs = [
        pltpu.make_async_copy(folded_ref.at[t], folded_hbm.at[t], out_sems.at[t])
        for t in range(3)
    ]
    for copy in ins:
        copy.start()

    row = iota((512, 512), 0)
    col = iota((512, 512), 1)
    lanes_ref[...] = one(col == (row & 3) * 128 + (row >> 6) * 16 + ((row >> 2) & 15))

    row = iota((256, 768), 0)
    col = iota((256, 768), 1)
    step = (col >> 4) & 3
    spread_ref[...] = one(
        (row >> 7 == (col >> 6) & 1)
        & (step < 3)
        & ((row >> 4) & 7 == (col >> 7) + step)
        & (row & 15 == col & 15)
    )

    stem_out_ref[...] = jnp.zeros(stem_out_ref.shape, BF16)
    for dy in range(3):
        for dx in range(3):
            stem_out_ref[dy, dx * 64 : dx * 64 + 48, :] = stem_ref[dy * 3 + dx]

    for t in range(3):
        ins[t].wait()

        def fold(part, carry, t=t):
            rows = pl.ds(pl.multiple_of(part * 32, 32), 32)
            by_row = []
            for w in range(3):
                w0, w1, w2 = (second_ref[t, u, w, rows, :].astype(F32) for u in range(3))
                by_row.append((w0, w1 + w2, w0 + w1, w2))
            for a in range(2):
                for ty in range(2):
                    c0, c1, c2 = (by_row[w][2 * a + ty] for w in range(3))
                    for b, tx, v in ((0, 0, c0), (0, 1, c1 + c2), (1, 0, c0 + c1), (1, 1, c2)):
                        folded_ref[t, a * 2 + b, ty * 2 + tx, rows, :] = v.astype(BF16)
            return carry

        lax.fori_loop(0, CH // 32, fold, 0)
        outs[t].start()
    for copy in outs:
        copy.wait()


def pick_kernel(own_ref, other_ref, pick_ref, out_ref, rows_ref):
    gap = jnp.zeros((64, 32), BF16)
    both = jnp.concatenate([own_ref[...], gap, other_ref[...], gap], axis=1)
    picked = lax.dot_general(
        pick_ref[...], both, (((1,), (1,)), ((), ())), preferred_element_type=F32
    )
    joined = jnp.concatenate([picked[:128], picked[128:]], axis=1)
    for part in range(8):
        rows_ref[pl.ds(part, SEQ, stride=8), :] = joined[part * SEQ : (part + 1) * SEQ]
    out_ref[...] = rows_ref[...].astype(BF16).reshape(out_ref.shape)


def silu(v):
    halved = 0.5 * v
    return halved + halved * jnp.tanh(halved)


def store_taps(ref, frame, y, value):
    split = value.reshape(2, 8, CH)
    column = iota((2, 8, CH), 1)
    before = jnp.where(column == 0, 0.0, pltpu.roll(split, 1, 1))
    after = jnp.where(column == 7, 0.0, pltpu.roll(split, 7, 1))
    ref[0, frame, y + 1] = before.reshape(16, CH).astype(BF16)
    ref[1, frame, y + 1] = value.astype(BF16)
    ref[2, frame, y + 1] = after.reshape(16, CH).astype(BF16)


def main_kernel(
    tokens_ref,
    place_ref,
    limits_ref,
    lanes_ref,
    spread_ref,
    stem_ref,
    stem_bias_ref,
    first_hbm,
    first_bias_ref,
    folded_hbm,
    second_bias_ref,
    out_ref,
    rows_ref,
    taps_ref,
    one_ref,
    two_ref,
    first_ref,
    folded_ref,
    mixed_ref,
    sems,
):
    copies = [
        pltpu.make_async_copy(first_hbm.at[u], first_ref.at[u], sems.at[u]) for u in range(3)
    ]
    fetches = [
        pltpu.make_async_copy(folded_hbm.at[t], folded_ref.at[t], sems.at[3 + t]) for t in range(3)
    ]
    for copy in copies + fetches:
        copy.start()

    rows_ref[...] = tokens_ref[...].reshape(128, 128).astype(F32)
    window = jnp.concatenate(
        [
            jnp.concatenate(
                [rows_ref[pl.ds(k * 4 + pair, SEQ, stride=8), :] for pair in range(4)], axis=1
            )
            for k in range(2)
        ],
        axis=0,
    ).astype(BF16)
    parity = jnp.dot(window, lanes_ref[...], preferred_element_type=F32).astype(BF16)
    stacked = jnp.concatenate([parity[:, n * 128 : (n + 1) * 128] for n in range(4)], axis=0)
    placed = jnp.dot(place_ref[...], stacked, preferred_element_type=F32).astype(BF16)
    near = jnp.dot(
        jnp.concatenate([placed[:128], placed[128:256]], axis=1),
        spread_ref[...],
        preferred_element_type=F32,
    ).astype(BF16)
    far = jnp.dot(
        placed[256:], spread_ref[:128], preferred_element_type=F32
    ).astype(BF16)
    zero_row = jnp.zeros((16, CH), BF16)
    for g in range(6):
        lanes = slice(g * 128, (g + 1) * 128)
        taps_ref[g, 0] = zero_row
        taps_ref[g, 1:9, :, :128] = near[:, lanes].reshape(8, 16, 128)
        taps_ref[g, 1:9, :, 128:] = far[:, lanes].reshape(8, 16, 128)
        taps_ref[g, 9] = zero_row
        for dx in range(3):
            one_ref[dx, g, 0] = zero_row
            one_ref[dx, g, 9] = zero_row
    for g in range(4):
        for dx in range(3):
            two_ref[dx, g, 0] = zero_row
            two_ref[dx, g, 9] = zero_row

    tall = limits_ref[0]
    wide = limits_ref[1]
    start = limits_ref[2]
    count = limits_ref[3]
    tall = jnp.concatenate([tall, tall], axis=1)
    wide = jnp.concatenate([wide, wide], axis=1)
    start = jnp.concatenate([start, start], axis=1)
    count = jnp.concatenate([count, count], axis=1)
    column = iota((16, CH), 0) & 7
    inside = column < wide

    def finish(frame, offset, y, total, bias, ref):
        value = silu(total + bias)
        keep = inside & (tall > y) & (start + offset + frame >= 0)
        store_taps(ref, frame, y, jnp.where(keep, value, 0.0))

    stem_bias = stem_bias_ref[...]
    hidden = jnp.dot(
        taps_ref[:, 0:8].reshape(768, CH), stem_ref[0], preferred_element_type=F32
    )
    for dy in range(1, 3):
        hidden = hidden + jnp.dot(
            taps_ref[:, dy : dy + 8].reshape(768, CH), stem_ref[dy], preferred_element_type=F32
        )
    hidden = hidden.reshape(6, 8, 16, CH)
    for g in range(6):
        for y in range(8):
            finish(g, 2, y, hidden[g, y], stem_bias, one_ref)

    first_bias = first_bias_ref[...]
    total = None
    for dy in range(3):
        copies[dy].wait()
        for dx in range(3):
            for dt in range(3):
                part = jnp.dot(
                    one_ref[dx, dt : dt + 4, dy : dy + 8].reshape(512, CH),
                    first_ref[dy, dx, dt],
                    preferred_element_type=F32,
                )
                total = part if total is None else total + part
    total = total.reshape(4, 8, 16, CH)
    for g in range(4):
        for y in range(8):
            finish(g, 4, y, total[g, y], first_bias, two_ref)

    for copy in fetches:
        copy.wait()
    second_bias = second_bias_ref[...]
    for a in range(2):
        for b in range(2):
            total = None
            for ty in range(2):
                for tx in range(2):
                    for dt in range(3):
                        part = jnp.dot(
                            two_ref[b + tx, dt : dt + 2, a + ty : a + ty + 8].reshape(256, CH),
                            folded_ref[dt, a * 2 + b, ty * 2 + tx],
                            preferred_element_type=F32,
                        )
                        total = part if total is None else total + part
            total = total.reshape(2, 8, 16, CH)
            for f in range(2):
                for y in range(8):
                    value = silu(total[f, y] + second_bias)
                    keep = inside & (tall > y) & (start + 6 + f < count)
                    value = jnp.where(keep, value, 0.0)
                    for k in range(2):
                        row = ((k * 2 + f) * 16 + 2 * y + a) * 16 + b
                        for side in range(2):
                            mixed_ref[side, pl.ds(row, 8, stride=2), :] = value[
                                k * 8 : k * 8 + 8, side * 128 : side * 128 + 128
                            ]
    for side in range(2):
        out_ref[:, side * 128 : side * 128 + 128] = mixed_ref[side].astype(BF16)


def held(value):
    return pltpu.with_memory_space_constraint(value, pltpu.VMEM)


def vmem_spec():
    return pl.BlockSpec(memory_space=pltpu.VMEM)


def hbm_spec():
    return pl.BlockSpec(memory_space=pl.ANY)


def fold(sent, stem_weight, second_weight):
    return pl.pallas_call(
        fold_kernel,
        out_shape=(
            pltpu.VMEM((512, 512), BF16),
            pltpu.VMEM((256, 768), BF16),
            pltpu.VMEM((3, 256, CH), BF16),
            jax.ShapeDtypeStruct((3, 4, 4, CH, CH), BF16),
        ),
        in_specs=[hbm_spec(), vmem_spec(), hbm_spec()],
        out_specs=(vmem_spec(),) * 3 + (hbm_spec(),),
        scratch_shapes=[
            pltpu.VMEM((3, 3, 3, CH, CH), BF16),
            pltpu.VMEM((3, 4, 4, CH, CH), BF16),
            pltpu.SemaphoreType.DMA((3,)),
            pltpu.SemaphoreType.DMA((3,)),
        ],
        compiler_params=pltpu.CompilerParams(vmem_limit_bytes=VMEM_LIMIT),
    )(sent, stem_weight.reshape(9, 48, CH), second_weight)


def decode(
    tokens, place, limits, lanes, spread, stem, stem_bias, first, first_bias, folded, second_bias
):
    return pl.pallas_call(
        main_kernel,
        out_shape=jax.ShapeDtypeStruct((1024, CH), BF16),
        in_specs=[vmem_spec()] * 7 + [hbm_spec(), vmem_spec(), hbm_spec(), vmem_spec()],
        out_specs=vmem_spec(),
        scratch_shapes=[
            pltpu.VMEM((128, 128), F32),
            pltpu.VMEM((6, 10, 16, CH), BF16),
            pltpu.VMEM((3, 6, 10, 16, CH), BF16),
            pltpu.VMEM((3, 4, 10, 16, CH), BF16),
            pltpu.VMEM((3, 3, 3, CH, CH), BF16),
            pltpu.VMEM((3, 4, 4, CH, CH), BF16),
            pltpu.VMEM((2, 1024, 128), F32),
            pltpu.SemaphoreType.DMA((6,)),
        ],
        compiler_params=pltpu.CompilerParams(vmem_limit_bytes=VMEM_LIMIT),
    )(
        tokens,
        place,
        limits,
        lanes,
        spread,
        stem,
        stem_bias[None],
        first,
        first_bias[None],
        folded,
        second_bias[None],
    )


def body(
    transformer_tokens,
    frames,
    heights,
    widths,
    tile_decode_device,
    tile_device_slot,
    stem_conv_weight,
    stem_conv_bias,
    upsample_first_weight,
    upsample_first_bias,
    upsample_second_weight,
    upsample_second_bias,
):
    requests = lax.axis_size("req")
    half = requests // 2
    own = jnp.transpose(transformer_tokens[0, :, 0, :])
    other = lax.ppermute(own, "req", [(i, (i + half) % requests) for i in range(requests)])
    shape = jax.ShapeDtypeStruct
    params = pltpu.CompilerParams(vmem_limit_bytes=60 * 1024 * 1024)
    pick, place, limits = pl.pallas_call(
        plan_kernel,
        out_shape=(
            pltpu.VMEM((256, 256), BF16),
            pltpu.VMEM((384, 128), BF16),
            pltpu.VMEM((4, 16, 128), I32),
        ),
        in_specs=[vmem_spec()] * 5,
        out_specs=(vmem_spec(),) * 3,
        compiler_params=params,
    )(
        frames[None],
        heights[None],
        widths[None],
        jnp.transpose(tile_decode_device, (2, 1, 0)),
        jnp.transpose(tile_device_slot, (2, 1, 0)),
    )
    sent = pl.pallas_call(
        pick_kernel,
        out_shape=shape((SEQ, 8, 128), BF16),
        in_specs=[vmem_spec()] * 3,
        out_specs=vmem_spec(),
        scratch_shapes=[pltpu.VMEM((128, 128), F32)],
    )(own, held(other), held(pick))
    tokens = lax.all_to_all(sent, "seq", 0, 0, tiled=True)
    lanes, spread, stem, folded = fold(sent, stem_conv_weight, upsample_second_weight)
    decoded = decode(
        held(tokens),
        held(place),
        held(limits),
        held(lanes),
        held(spread),
        held(stem),
        stem_conv_bias,
        upsample_first_weight,
        upsample_first_bias,
        folded,
        upsample_second_bias,
    )
    return decoded.reshape(1, 1, 2, 2, 16, 16, CH)


def solution(mesh):
    placed = (P("req", None, "seq", None), P(), P(), P(), P(), P(), P(), P(), P(), P(), P(), P())
    return jax.shard_map(
        body,
        mesh=mesh,
        in_specs=placed,
        out_specs=P("req", "seq", None, None, None, None, None),
        check_vma=False,
    )
```

```python
import functools

import jax
import jax.numpy as jnp
from jax import lax
from jax.experimental import pallas as pl
from jax.experimental.pallas import tpu as pltpu
from jax.sharding import PartitionSpec as P

F32 = jnp.float32
BF16 = jnp.bfloat16
I32 = jnp.int32
CH = 256
SEQ = 16
TILES = 3
VMEM_LIMIT = 52 * 1024 * 1024


def iota(shape, dim):
    return lax.broadcasted_iota(I32, shape, dim)


def one(mask):
    return jnp.where(mask, 1.0, 0.0).astype(BF16)


def plan_kernel(
    frames_ref,
    heights_ref,
    widths_ref,
    device_ref,
    slot_ref,
    pick_ref,
    place_ref,
):
    me = lax.axis_index("req")
    column = lax.axis_index("seq")
    half = frames_ref.shape[1] // 2
    partner = lax.rem(me + half, 2 * half)

    lane = iota((1, 32), 1)

    def entry(ref, who):
        return jnp.sum(jnp.where(lane == who, ref[...], 0), axis=1, keepdims=True)

    dest = iota((SEQ, 1), 0)
    tile_lane = iota((SEQ, 32), 1)

    def of_request(ref, tile, who):
        return jnp.sum(jnp.where(tile_lane == who, ref[tile], 0), axis=1, keepdims=True)

    codes = []
    lims = []
    tops = []
    for k in range(2):
        code = jnp.zeros((SEQ, 1), I32)
        live = jnp.zeros((SEQ, 1), I32)
        taken = jnp.zeros((SEQ, 1), I32)
        for i in range(TILES):
            start = 32 * i + 2 * dest - 6
            for who, offset in ((me, 0), (partner, 128)):
                hit = (of_request(device_ref, i, who) == me) & (
                    of_request(slot_ref, i, who) == k
                )
                code = code + jnp.where(hit, start + offset, 0)
                live = live + jnp.where(hit, 1, 0)
                if offset:
                    taken = taken + jnp.where(hit, 1, 0)
        lim = jnp.where(
            taken > 0,
            128 + entry(frames_ref, partner),
            jnp.where(live > 0, entry(frames_ref, me), 0),
        )
        code = jnp.where(live > 0, code, -64)
        codes.append(code)
        lims.append(lim)
        mine = dest == column

        def at_mine(v, mine=mine):
            return jnp.sum(jnp.where(mine, v, 0), axis=0, keepdims=True)

        my_taken = at_mine(taken) > 0
        my_live = at_mine(live) > 0
        tops.append(
            (
                jnp.where(my_taken, entry(heights_ref, partner), entry(heights_ref, me)),
                jnp.where(my_taken, entry(widths_ref, partner), entry(widths_ref, me)),
                at_mine(code) - jnp.where(my_taken, 128, 0),
                jnp.where(
                    my_live,
                    jnp.where(my_taken, entry(frames_ref, partner), entry(frames_ref, me)),
                    -64,
                ),
            )
        )

    source = iota((SEQ, 256), 1)
    for h in range(2):
        for k in range(2):
            for pair in range(4):
                row = (h * 8 + k * 4 + pair) * SEQ
                pick_ref[row : row + SEQ, :] = one(
                    (source == codes[k] + (2 * pair + h)) & (source < lims[k])
                )

    second_slot = iota((16, 128), 0) >= 8
    for n in range(4):
        place_ref[384 + 16 * n : 400 + 16 * n, :] = (
            jnp.where(second_slot, tops[1][n], tops[0][n]).astype(F32).astype(BF16)
        )

    row = iota((384, 128), 0)
    col = iota((384, 128), 1)
    tap = row >> 7
    y = (row >> 4) & 7
    which = (row >> 3) & 1
    x = (row & 7) + tap - 1
    tall = jnp.where(which == 1, tops[1][0], tops[0][0])
    wide = jnp.where(which == 1, tops[1][1], tops[0][1])
    wanted = ((y & 1) * 2 + (x & 1)) * 32 + which * 16 + (y >> 1) * 4 + (x >> 1)
    place_ref[:384, :] = one((col == wanted) & (y < tall) & (x >= 0) & (x < wide))


def constants_kernel(sent_hbm, stem_ref, lanes_ref, spread_ref, stem_out_ref):
    row = iota((512, 512), 0)
    col = iota((512, 512), 1)
    lanes_ref[...] = one(col == (row & 3) * 128 + (row >> 6) * 16 + ((row >> 2) & 15))

    row = iota((256, 768), 0)
    col = iota((256, 768), 1)
    step = (col >> 4) & 3
    spread_ref[...] = one(
        (row >> 7 == (col >> 6) & 1)
        & (step < 3)
        & ((row >> 4) & 7 == (col >> 7) + step)
        & (row & 15 == col & 15)
    )

    stem_out_ref[...] = jnp.zeros(stem_out_ref.shape, BF16)
    for dy in range(3):
        for dx in range(3):
            stem_out_ref[dy, dx * 64 : dx * 64 + 48, :] = stem_ref[dy * 3 + dx]


def fold_kernel(second_hbm, held_ref, folded_hbm, second_ref, folded_ref, in_sems, out_sems):
    ins = [
        pltpu.make_async_copy(second_hbm.at[:, :, t], second_ref.at[t], in_sems.at[t])
        for t in range(3)
    ]
    outs = [
        pltpu.make_async_copy(folded_ref.at[t], folded_hbm.at[t], out_sems.at[t])
        for t in range(2)
    ]
    for t in (1, 2, 0):
        ins[t].start()

    for t in (1, 2, 0):
        ins[t].wait()

        def fold(part, carry, t=t):
            rows = pl.ds(pl.multiple_of(part * 32, 32), 32)
            by_row = []
            for w in range(3):
                w0, w1, w2 = (second_ref[t, u, w, rows, :].astype(F32) for u in range(3))
                by_row.append((w0, w1 + w2, w0 + w1, w2))
            for a in range(2):
                for ty in range(2):
                    c0, c1, c2 = (by_row[w][2 * a + ty] for w in range(3))
                    for b, tx, v in ((0, 0, c0), (0, 1, c1 + c2), (1, 0, c0 + c1), (1, 1, c2)):
                        if t:
                            folded_ref[t - 1, a * 2 + b, ty * 2 + tx, rows, :] = v.astype(BF16)
                        else:
                            held_ref[a * 2 + b, ty * 2 + tx, rows, :] = v.astype(BF16)
            return carry

        lax.fori_loop(0, CH // 32, fold, 0)
        if t:
            outs[t - 1].start()
    for copy in outs:
        copy.wait()


def pick_kernel(own_ref, other_ref, pick_ref, folded_hbm, out_ref, rows_ref):
    gap = jnp.zeros((64, 32), BF16)
    both = jnp.concatenate([own_ref[...], gap, other_ref[...], gap], axis=1)
    picked = lax.dot_general(
        pick_ref[...], both, (((1,), (1,)), ((), ())), preferred_element_type=F32
    )
    joined = jnp.concatenate([picked[:128], picked[128:]], axis=1)
    for part in range(8):
        rows_ref[pl.ds(part, SEQ, stride=8), :] = joined[part * SEQ : (part + 1) * SEQ]
    out_ref[...] = rows_ref[...].astype(BF16).reshape(out_ref.shape)


def silu(v):
    halved = 0.5 * v
    return halved + halved * jnp.tanh(halved)


def store_taps(ref, frame, y, value):
    split = value.reshape(2, 8, CH)
    column = iota((2, 8, CH), 1)
    before = jnp.where(column == 0, 0.0, pltpu.roll(split, 1, 1))
    after = jnp.where(column == 7, 0.0, pltpu.roll(split, 7, 1))
    ref[0, frame, y + 1] = before.reshape(16, CH).astype(BF16)
    ref[1, frame, y + 1] = value.astype(BF16)
    ref[2, frame, y + 1] = after.reshape(16, CH).astype(BF16)


def multiply(work):
    for m, steps in enumerate(work):
        pltpu.matmul_push_rhs(steps[0][0](), 0, m)
    for n in range(max(len(steps) for steps in work)):
        for m, steps in enumerate(work):
            if n + 1 < len(steps):
                pltpu.matmul_push_rhs(steps[n + 1][0](), (n + 1) % 2, m)
            if n < len(steps):
                for order, (acc, rows) in enumerate(steps[n][1]):
                    pltpu.matmul_acc_lhs(acc, rows(), load_staged_rhs=n % 2 if order == 0 else None)


def main_body(
    tokens_ref,
    place_ref,
    lanes_ref,
    spread_ref,
    stem_ref,
    stem_bias_ref,
    first_hbm,
    first_bias_ref,
    folded_ready_ref,
    folded_hbm,
    second_bias_ref,
    out_ref,
    rows_ref,
    taps_ref,
    one_ref,
    two_ref,
    first_ref,
    folded_ref,
    mixed_ref,
    sems,
    *accs,
):
    accs, small = (accs[:4], accs[4:8]), accs[8:]
    copies = [
        pltpu.make_async_copy(first_hbm.at[u], first_ref.at[u], sems.at[u]) for u in range(3)
    ]
    fetches = [
        pltpu.make_async_copy(folded_hbm.at[t], folded_ref.at[t], sems.at[3 + t]) for t in range(2)
    ]
    for copy in copies + fetches:
        copy.start()

    rows_ref[...] = tokens_ref[...].reshape(128, 128).astype(F32)
    window = jnp.concatenate(
        [
            jnp.concatenate(
                [rows_ref[pl.ds(k * 4 + pair, SEQ, stride=8), :] for pair in range(4)], axis=1
            )
            for k in range(2)
        ],
        axis=0,
    ).astype(BF16)
    multiply(
        [
            [
                (
                    lambda m=m, k=k: lanes_ref[k * CH : k * CH + CH, m * CH : m * CH + CH],
                    [(small[m], lambda k=k: window[:, k * CH : k * CH + CH])],
                )
                for k in range(2)
            ]
            for m in range(2)
        ]
    )
    parity = [pltpu.matmul_pop(small[m]).astype(BF16) for m in range(2)]
    blank = jnp.zeros((128, 128), BF16)
    stacked = jnp.concatenate(
        [parity[n // 2][:, n % 2 * 128 : n % 2 * 128 + 128] for n in range(4)], axis=0
    )
    stacked = jnp.concatenate(
        [jnp.concatenate([stacked, blank], axis=1), jnp.zeros((128, CH), BF16)], axis=0
    )
    multiply(
        [
            [
                (
                    lambda: stacked,
                    [
                        (
                            accs[m][n],
                            lambda t=2 * m + n: jnp.concatenate(
                                [place_ref[t * 128 : t * 128 + 128], blank], axis=1
                            ),
                        )
                        for n in range(2 - m)
                    ],
                )
            ]
            for m in range(2)
        ]
    )
    placed = [
        pltpu.matmul_pop(acc)[:, :128].astype(BF16) for acc in (accs[0][0], accs[0][1], accs[1][0])
    ]
    joined = (
        jnp.concatenate(placed[:2], axis=1),
        jnp.concatenate([placed[2], blank], axis=1),
    )
    multiply(
        [
            [
                (
                    lambda t=t: spread_ref[:, t * CH : t * CH + CH],
                    [(accs[m][t // 2 * 2 + n], lambda n=n: joined[n]) for n in range(2)],
                )
                for t in range(m, 3, 2)
            ]
            for m in range(2)
        ]
    )
    spread_out = [
        [pltpu.matmul_pop(accs[t % 2][t // 2 * 2 + n]).astype(BF16) for n in range(2)] for t in range(3)
    ]
    zero_row = jnp.zeros((16, CH), BF16)
    for g in range(6):
        lanes = slice(g % 2 * 128, g % 2 * 128 + 128)
        near, far = spread_out[g // 2]
        taps_ref[g, 0] = zero_row
        taps_ref[g, 1:9, :, :128] = near[:, lanes].reshape(8, 16, 128)
        taps_ref[g, 1:9, :, 128:] = far[:, lanes].reshape(8, 16, 128)
        taps_ref[g, 9] = zero_row
        for dx in range(3):
            one_ref[dx, g, 0] = zero_row
            one_ref[dx, g, 9] = zero_row
    for g in range(4):
        for dx in range(3):
            two_ref[dx, g, 0] = zero_row
            two_ref[dx, g, 9] = zero_row

    tall, wide, start, count = (
        place_ref[384 + 16 * n : 400 + 16 * n, :].astype(F32).astype(I32) for n in range(4)
    )
    tall = jnp.concatenate([tall, tall], axis=1)
    wide = jnp.concatenate([wide, wide], axis=1)
    start = jnp.concatenate([start, start], axis=1)
    count = jnp.concatenate([count, count], axis=1)
    column = iota((16, CH), 0) & 7
    inside = column < wide

    def finish(frame, offset, y, total, bias, ref):
        value = silu(total + bias)
        keep = inside & (tall > y) & (start + offset + frame >= 0)
        store_taps(ref, frame, y, jnp.where(keep, value, 0.0))

    stem_bias = stem_bias_ref[...]
    multiply(
        [
            [
                (
                    lambda dy=dy: stem_ref[dy],
                    [
                        (accs[m][n], lambda g=3 * m + n, dy=dy: taps_ref[g, dy : dy + 8].reshape(128, CH))
                        for n in range(3)
                    ],
                )
                for dy in range(3)
            ]
            for m in range(2)
        ]
    )
    for n in range(3):
        for m in range(2):
            hidden = pltpu.matmul_pop(accs[m][n]).reshape(8, 16, CH)
            for y in range(8):
                finish(3 * m + n, 2, y, hidden[y], stem_bias, one_ref)

    first_bias = first_bias_ref[...]
    for dy in range(3):
        copies[dy].wait()
    taps = [(dy, dx, dt) for dy in range(3) for dx in range(3) for dt in range(3)]
    multiply(
        [
            [
                (
                    lambda tap=tap: first_ref[tap],
                    [
                        (
                            accs[m][n],
                            lambda n=n, tap=tap: one_ref[
                                tap[1], tap[2] + n, tap[0] : tap[0] + 8
                            ].reshape(128, CH),
                        )
                        for n in range(4)
                    ],
                )
                for tap in taps[m::2]
            ]
            for m in range(2)
        ]
    )
    for g in range(4):
        total = pltpu.matmul_pop(accs[0][g]) + pltpu.matmul_pop(accs[1][g])
        total = total.reshape(8, 16, CH)
        for y in range(8):
            finish(g, 4, y, total[y], first_bias, two_ref)

    for copy in fetches:
        copy.wait()
    second_bias = second_bias_ref[...]
    for b in range(2):
        multiply(
            [
                [
                    (
                        lambda a=a, b=b, ty=ty, tx=tx, dt=dt: (
                            folded_ref.at[dt - 1] if dt else folded_ready_ref
                        )[a * 2 + b, ty * 2 + tx],
                        [
                            (
                                accs[a][2 * b + f],
                                lambda f=f, a=a, b=b, ty=ty, tx=tx, dt=dt: two_ref[
                                    b + tx, dt + f, a + ty : a + ty + 8
                                ].reshape(128, CH),
                            )
                            for f in range(2)
                        ],
                    )
                    for ty in range(2)
                    for tx in range(2)
                    for dt in range(3)
                ]
                for a in range(2)
            ]
        )
    for b in range(2):
        for a in range(2):
            for f in range(2):
                total = pltpu.matmul_pop(accs[a][2 * b + f]).reshape(8, 16, CH)
                for y in range(8):
                    value = silu(total[y] + second_bias)
                    keep = inside & (tall > y) & (start + 6 + f < count)
                    value = jnp.where(keep, value, 0.0)
                    for k in range(2):
                        row = ((k * 2 + f) * 16 + 2 * y + a) * 16 + b
                        for side in range(2):
                            mixed_ref[side, pl.ds(row, 8, stride=2), :] = value[
                                k * 8 : k * 8 + 8, side * 128 : side * 128 + 128
                            ]
    for side in range(2):
        out_ref[:, side * 128 : side * 128 + 128] = mixed_ref[side].astype(BF16)


def main_kernel(*refs):
    pl.run_scoped(
        functools.partial(main_body, *refs),
        *[pltpu.ACC(m)((128, CH), F32) for m in range(2) for _ in range(4)],
        *[pltpu.ACC(m)((32, CH), F32) for m in range(2)],
    )


def held(value):
    return pltpu.with_memory_space_constraint(value, pltpu.VMEM)


def vmem_spec():
    return pl.BlockSpec(memory_space=pltpu.VMEM)


def hbm_spec():
    return pl.BlockSpec(memory_space=pl.ANY)


def fold(second_weight):
    return pl.pallas_call(
        fold_kernel,
        out_shape=(
            pltpu.VMEM((4, 4, CH, CH), BF16),
            jax.ShapeDtypeStruct((2, 4, 4, CH, CH), BF16),
        ),
        in_specs=[hbm_spec()],
        out_specs=(vmem_spec(), hbm_spec()),
        scratch_shapes=[
            pltpu.VMEM((3, 3, 3, CH, CH), BF16),
            pltpu.VMEM((2, 4, 4, CH, CH), BF16),
            pltpu.SemaphoreType.DMA((3,)),
            pltpu.SemaphoreType.DMA((2,)),
        ],
        compiler_params=pltpu.CompilerParams(vmem_limit_bytes=VMEM_LIMIT),
    )(second_weight)


def constants(sent, stem_weight):
    return pl.pallas_call(
        constants_kernel,
        out_shape=(
            pltpu.VMEM((512, 512), BF16),
            pltpu.VMEM((256, 768), BF16),
            pltpu.VMEM((3, 256, CH), BF16),
        ),
        in_specs=[hbm_spec(), vmem_spec()],
        out_specs=(vmem_spec(),) * 3,
        compiler_params=pltpu.CompilerParams(vmem_limit_bytes=VMEM_LIMIT),
    )(sent, stem_weight.reshape(9, 48, CH))


def decode(
    tokens,
    place,
    lanes,
    spread,
    stem,
    stem_bias,
    first,
    first_bias,
    ready,
    folded,
    second_bias,
):
    return pl.pallas_call(
        main_kernel,
        out_shape=jax.ShapeDtypeStruct((1024, CH), BF16),
        in_specs=[vmem_spec()] * 6
        + [hbm_spec(), vmem_spec(), vmem_spec(), hbm_spec(), vmem_spec()],
        out_specs=vmem_spec(),
        scratch_shapes=[
            pltpu.VMEM((128, 128), F32),
            pltpu.VMEM((6, 10, 16, CH), BF16),
            pltpu.VMEM((3, 6, 10, 16, CH), BF16),
            pltpu.VMEM((3, 4, 10, 16, CH), BF16),
            pltpu.VMEM((3, 3, 3, CH, CH), BF16),
            pltpu.VMEM((2, 4, 4, CH, CH), BF16),
            pltpu.VMEM((2, 1024, 128), F32),
            pltpu.SemaphoreType.DMA((5,)),
        ],
        compiler_params=pltpu.CompilerParams(vmem_limit_bytes=VMEM_LIMIT),
    )(
        tokens,
        place,
        lanes,
        spread,
        stem,
        stem_bias[None],
        first,
        first_bias[None],
        ready,
        folded,
        second_bias[None],
    )


def body(
    transformer_tokens,
    frames,
    heights,
    widths,
    tile_decode_device,
    tile_device_slot,
    stem_conv_weight,
    stem_conv_bias,
    upsample_first_weight,
    upsample_first_bias,
    upsample_second_weight,
    upsample_second_bias,
):
    requests = lax.axis_size("req")
    half = requests // 2
    own = jnp.transpose(transformer_tokens[0, :, 0, :])
    other = lax.ppermute(own, "req", [(i, (i + half) % requests) for i in range(requests)])
    shape = jax.ShapeDtypeStruct
    params = pltpu.CompilerParams(vmem_limit_bytes=60 * 1024 * 1024)
    pick, place = pl.pallas_call(
        plan_kernel,
        out_shape=(
            pltpu.VMEM((256, 256), BF16),
            pltpu.VMEM((448, 128), BF16),
        ),
        in_specs=[vmem_spec()] * 5,
        out_specs=(vmem_spec(),) * 2,
        compiler_params=params,
    )(
        frames[None],
        heights[None],
        widths[None],
        jnp.transpose(tile_decode_device, (2, 1, 0)),
        jnp.transpose(tile_device_slot, (2, 1, 0)),
    )
    ready, folded = fold(upsample_second_weight)
    sent = pl.pallas_call(
        pick_kernel,
        out_shape=pltpu.VMEM((SEQ, 8, 128), BF16),
        in_specs=[vmem_spec()] * 3 + [hbm_spec()],
        out_specs=vmem_spec(),
        scratch_shapes=[pltpu.VMEM((128, 128), F32)],
        compiler_params=pltpu.CompilerParams(vmem_limit_bytes=VMEM_LIMIT),
    )(held(own), held(other), held(pick), folded)
    tokens = lax.all_to_all(sent, "seq", 0, 0, tiled=True)
    lanes, spread, stem = constants(sent, stem_conv_weight)
    decoded = decode(
        held(tokens),
        held(place),
        held(lanes),
        held(spread),
        held(stem),
        stem_conv_bias,
        upsample_first_weight,
        upsample_first_bias,
        held(ready),
        folded,
        upsample_second_bias,
    )
    return decoded.reshape(1, 1, 2, 2, 16, 16, CH)


def solution(mesh):
    placed = (P("req", None, "seq", None), P(), P(), P(), P(), P(), P(), P(), P(), P(), P(), P())
    return jax.shard_map(
        body,
        mesh=mesh,
        in_specs=placed,
        out_specs=P("req", "seq", None, None, None, None, None),
        check_vma=False,
    )
```

```python
import functools

import jax
import jax.numpy as jnp
from jax import lax
from jax.experimental import pallas as pl
from jax.experimental.pallas import tpu as pltpu
from jax.sharding import PartitionSpec as P

F32 = jnp.float32
BF16 = jnp.bfloat16
I32 = jnp.int32
CH = 256
SEQ = 16
TILES = 3
EARLY = 15
VMEM_LIMIT = 52 * 1024 * 1024


def iota(shape, dim):
    return lax.broadcasted_iota(I32, shape, dim)


def one(mask):
    return jnp.where(mask, 1.0, 0.0).astype(BF16)


def plan_kernel(
    frames_ref,
    heights_ref,
    widths_ref,
    device_ref,
    slot_ref,
    pick_ref,
    place_ref,
):
    me = lax.axis_index("req")
    column = lax.axis_index("seq")
    half = frames_ref.shape[1] // 2
    partner = lax.rem(me + half, 2 * half)

    lane = iota((1, 32), 1)

    def entry(ref, who):
        return jnp.sum(jnp.where(lane == who, ref[...], 0), axis=1, keepdims=True)

    dest = iota((SEQ, 1), 0)
    tile_lane = iota((SEQ, 32), 1)

    def of_request(ref, tile, who):
        return jnp.sum(jnp.where(tile_lane == who, ref[tile], 0), axis=1, keepdims=True)

    codes = []
    lims = []
    tops = []
    for k in range(2):
        code = jnp.zeros((SEQ, 1), I32)
        live = jnp.zeros((SEQ, 1), I32)
        taken = jnp.zeros((SEQ, 1), I32)
        for i in range(TILES):
            start = 32 * i + 2 * dest - 6
            for who, offset in ((me, 0), (partner, 128)):
                hit = (of_request(device_ref, i, who) == me) & (
                    of_request(slot_ref, i, who) == k
                )
                code = code + jnp.where(hit, start + offset, 0)
                live = live + jnp.where(hit, 1, 0)
                if offset:
                    taken = taken + jnp.where(hit, 1, 0)
        lim = jnp.where(
            taken > 0,
            128 + entry(frames_ref, partner),
            jnp.where(live > 0, entry(frames_ref, me), 0),
        )
        code = jnp.where(live > 0, code, -64)
        codes.append(code)
        lims.append(lim)
        mine = dest == column

        def at_mine(v, mine=mine):
            return jnp.sum(jnp.where(mine, v, 0), axis=0, keepdims=True)

        my_taken = at_mine(taken) > 0
        my_live = at_mine(live) > 0
        tops.append(
            (
                jnp.where(my_taken, entry(heights_ref, partner), entry(heights_ref, me)),
                jnp.where(my_taken, entry(widths_ref, partner), entry(widths_ref, me)),
                at_mine(code) - jnp.where(my_taken, 128, 0),
                jnp.where(
                    my_live,
                    jnp.where(my_taken, entry(frames_ref, partner), entry(frames_ref, me)),
                    -64,
                ),
            )
        )

    source = iota((SEQ, 256), 1)
    for h in range(2):
        for k in range(2):
            for pair in range(4):
                row = (h * 8 + k * 4 + pair) * SEQ
                pick_ref[row : row + SEQ, :] = one(
                    (source == codes[k] + (2 * pair + h)) & (source < lims[k])
                )

    second_slot = iota((16, 128), 0) >= 8
    for n in range(4):
        place_ref[384 + 16 * n : 400 + 16 * n, :] = (
            jnp.where(second_slot, tops[1][n], tops[0][n]).astype(F32).astype(BF16)
        )

    row = iota((384, 128), 0)
    col = iota((384, 128), 1)
    tap = row >> 7
    y = (row >> 4) & 7
    which = (row >> 3) & 1
    x = (row & 7) + tap - 1
    tall = jnp.where(which == 1, tops[1][0], tops[0][0])
    wide = jnp.where(which == 1, tops[1][1], tops[0][1])
    wanted = ((y & 1) * 2 + (x & 1)) * 32 + which * 16 + (y >> 1) * 4 + (x >> 1)
    place_ref[:384, :] = one((col == wanted) & (y < tall) & (x >= 0) & (x < wide))


def constants_kernel(
    sent_hbm, stem_ref, first_hbm, lanes_ref, spread_ref, stem_out_ref, ready_ref, sem
):
    early = pltpu.make_async_copy(first_hbm.at[:EARLY], ready_ref, sem)
    early.start()
    row = iota((512, 512), 0)
    col = iota((512, 512), 1)
    lanes_ref[...] = one(col == (row & 3) * 128 + (row >> 6) * 16 + ((row >> 2) & 15))

    row = iota((256, 768), 0)
    col = iota((256, 768), 1)
    step = (col >> 4) & 3
    spread_ref[...] = one(
        (row >> 7 == (col >> 6) & 1)
        & (step < 3)
        & ((row >> 4) & 7 == (col >> 7) + step)
        & (row & 15 == col & 15)
    )

    stem_out_ref[...] = jnp.zeros(stem_out_ref.shape, BF16)
    for dy in range(3):
        for dx in range(3):
            stem_out_ref[dy, dx * 64 : dx * 64 + 48, :] = stem_ref[dy * 3 + dx]
    early.wait()


def pick_kernel(own_ref, other_ref, pick_ref, out_ref, rows_ref):
    gap = jnp.zeros((64, 32), BF16)
    both = jnp.concatenate([own_ref[...], gap, other_ref[...], gap], axis=1)
    picked = lax.dot_general(
        pick_ref[...], both, (((1,), (1,)), ((), ())), preferred_element_type=F32
    )
    joined = jnp.concatenate([picked[:128], picked[128:]], axis=1)
    for part in range(8):
        rows_ref[pl.ds(part, SEQ, stride=8), :] = joined[part * SEQ : (part + 1) * SEQ]
    out_ref[...] = rows_ref[...].astype(BF16).reshape(out_ref.shape)


def silu(v):
    halved = 0.5 * v
    return halved + halved * jnp.tanh(halved)


def store_taps(ref, frame, y, value):
    split = value.reshape(2, 8, CH)
    column = iota((2, 8, CH), 1)
    before = jnp.where(column == 0, 0.0, pltpu.roll(split, 1, 1))
    after = jnp.where(column == 7, 0.0, pltpu.roll(split, 7, 1))
    ref[0, frame, y + 1] = before.reshape(16, CH).astype(BF16)
    ref[1, frame, y + 1] = value.astype(BF16)
    ref[2, frame, y + 1] = after.reshape(16, CH).astype(BF16)


def multiply(work, beside=()):
    for m, steps in enumerate(work):
        pltpu.matmul_push_rhs(steps[0][0](), 0, m)
    for n in range(max(len(steps) for steps in work)):
        for m, steps in enumerate(work):
            if n + 1 < len(steps):
                pltpu.matmul_push_rhs(steps[n + 1][0](), (n + 1) % 2, m)
            if n < len(steps):
                for order, (acc, rows) in enumerate(steps[n][1]):
                    pltpu.matmul_acc_lhs(acc, rows(), load_staged_rhs=n % 2 if order == 0 else None)
        for step, thunk in beside:
            if step == n:
                thunk()


def main_body(
    tokens_ref,
    place_ref,
    lanes_ref,
    spread_ref,
    stem_ref,
    stem_bias_ref,
    ready_ref,
    first_hbm,
    first_bias_ref,
    second_hbm,
    second_bias_ref,
    out_ref,
    rows_ref,
    taps_ref,
    one_ref,
    two_ref,
    first_ref,
    second_ref,
    folded_ref,
    mixed_ref,
    sems,
    *accs,
):
    accs, small = (accs[:4], accs[4:8]), accs[8:]
    copies = [pltpu.make_async_copy(first_hbm.at[EARLY:], first_ref, sems.at[3])]
    fetches = [
        pltpu.make_async_copy(second_hbm.at[:, :, t], second_ref.at[t], sems.at[t]) for t in range(3)
    ]
    for copy in copies + fetches:
        copy.start()

    rows_ref[...] = tokens_ref[...].reshape(128, 128).astype(F32)
    window = jnp.concatenate(
        [
            jnp.concatenate(
                [rows_ref[pl.ds(k * 4 + pair, SEQ, stride=8), :] for pair in range(4)], axis=1
            )
            for k in range(2)
        ],
        axis=0,
    ).astype(BF16)
    multiply(
        [
            [
                (
                    lambda m=m, k=k: lanes_ref[k * CH : k * CH + CH, m * CH : m * CH + CH],
                    [(small[m], lambda k=k: window[:, k * CH : k * CH + CH])],
                )
                for k in range(2)
            ]
            for m in range(2)
        ]
    )
    parity = [pltpu.matmul_pop(small[m]).astype(BF16) for m in range(2)]
    blank = jnp.zeros((128, 128), BF16)
    stacked = jnp.concatenate(
        [parity[n // 2][:, n % 2 * 128 : n % 2 * 128 + 128] for n in range(4)], axis=0
    )
    stacked = jnp.concatenate(
        [jnp.concatenate([stacked, blank], axis=1), jnp.zeros((128, CH), BF16)], axis=0
    )
    multiply(
        [
            [
                (
                    lambda: stacked,
                    [
                        (
                            accs[m][n],
                            lambda t=2 * m + n: jnp.concatenate(
                                [place_ref[t * 128 : t * 128 + 128], blank], axis=1
                            ),
                        )
                        for n in range(2 - m)
                    ],
                )
            ]
            for m in range(2)
        ]
    )
    placed = [
        pltpu.matmul_pop(acc)[:, :128].astype(BF16) for acc in (accs[0][0], accs[0][1], accs[1][0])
    ]
    joined = (
        jnp.concatenate(placed[:2], axis=1),
        jnp.concatenate([placed[2], blank], axis=1),
    )
    multiply(
        [
            [
                (
                    lambda t=t: spread_ref[:, t * CH : t * CH + CH],
                    [(accs[m][t // 2 * 2 + n], lambda n=n: joined[n]) for n in range(2)],
                )
                for t in range(m, 3, 2)
            ]
            for m in range(2)
        ]
    )
    spread_out = [
        [pltpu.matmul_pop(accs[t % 2][t // 2 * 2 + n]).astype(BF16) for n in range(2)] for t in range(3)
    ]
    zero_row = jnp.zeros((16, CH), BF16)
    for g in range(6):
        lanes = slice(g % 2 * 128, g % 2 * 128 + 128)
        near, far = spread_out[g // 2]
        taps_ref[g, 0] = zero_row
        taps_ref[g, 1:9, :, :128] = near[:, lanes].reshape(8, 16, 128)
        taps_ref[g, 1:9, :, 128:] = far[:, lanes].reshape(8, 16, 128)
        taps_ref[g, 9] = zero_row
        for dx in range(3):
            one_ref[dx, g, 0] = zero_row
            one_ref[dx, g, 9] = zero_row
    for g in range(4):
        for dx in range(3):
            two_ref[dx, g, 0] = zero_row
            two_ref[dx, g, 9] = zero_row

    tall, wide, start, count = (
        place_ref[384 + 16 * n : 400 + 16 * n, :].astype(F32).astype(I32) for n in range(4)
    )
    tall = jnp.where((iota((16, 128), 0) & 7) < wide, tall, 0)

    def limit(keep):
        rows = jnp.where(keep, tall, 0)
        return jnp.concatenate([rows, rows], axis=1)

    def finish(frame, rows, y, total, bias, ref):
        store_taps(ref, frame, y, jnp.where(rows > y, silu(total + bias), 0.0))

    stem_bias = stem_bias_ref[...]
    multiply(
        [
            [
                (
                    lambda dy=dy: stem_ref[dy],
                    [
                        (accs[m][n], lambda g=3 * m + n, dy=dy: taps_ref[g, dy : dy + 8].reshape(128, CH))
                        for n in range(3)
                    ],
                )
                for dy in range(3)
            ]
            for m in range(2)
        ]
    )
    for n in range(3):
        for m in range(2):
            hidden = pltpu.matmul_pop(accs[m][n]).reshape(8, 16, CH)
            rows = limit(start + (2 + 3 * m + n) >= 0)
            for y in range(8):
                finish(3 * m + n, rows, y, hidden[y], stem_bias, one_ref)

    first_bias = first_bias_ref[...]
    taps = [(dy, dx, dt) for dy in range(3) for dx in range(3) for dt in range(3)]
    corners = {(0, 0, 0, 0): (0, 0), (0, 1, 0, 1): (0, 2), (1, 0, 1, 0): (2, 0), (1, 1, 1, 1): (2, 2)}
    sums = [
        key
        for key in ((a, b, ty, tx) for a in range(2) for b in range(2) for ty in range(2) for tx in range(2))
        if key not in corners
    ]

    def fold(t):
        fetches[t].wait()
        for part in range(0, CH, 64):
            rows = slice(part, part + 64)
            w = [[second_ref[t, u, v, rows, :] for v in range(3)] for u in range(3)]
            by_row = [
                (w[0][v], w[1][v] + w[2][v], w[0][v] + w[1][v], w[2][v]) for v in range(3)
            ]
            for place, (a, b, ty, tx) in enumerate(sums):
                c = [by_row[v][2 * a + ty] for v in range(3)]
                folded_ref[t, place, rows, :] = (c[0], c[1] + c[2], c[0] + c[1], c[2])[2 * b + tx]

    def weights_of(t, *key):
        if key in corners:
            return second_ref[(t,) + corners[key]]
        return folded_ref[t, sums.index(key)]

    def first_weights(tap):
        place = tap[0] * 9 + tap[1] * 3 + tap[2]
        if place == EARLY:
            copies[0].wait()
        return ready_ref[place] if place < EARLY else first_ref[place - EARLY]

    multiply(
        [
            [
                (
                    lambda tap=tap: first_weights(tap),
                    [
                        (
                            accs[m][n],
                            lambda n=n, tap=tap: one_ref[
                                tap[1], tap[2] + n, tap[0] : tap[0] + 8
                            ].reshape(128, CH),
                        )
                        for n in range(4)
                    ],
                )
                for tap in taps[m::2]
            ]
            for m in range(2)
        ],
    )
    for t in range(3):
        fold(t)
    for g in range(4):
        total = pltpu.matmul_pop(accs[0][g]) + pltpu.matmul_pop(accs[1][g])
        total = total.reshape(8, 16, CH)
        rows = limit(start + (4 + g) >= 0)
        for y in range(8):
            finish(g, rows, y, total[y], first_bias, two_ref)

    second_bias = second_bias_ref[...]
    own_rows = [limit(start + (6 + f) < count) for f in range(2)]
    for b in range(2):
        multiply(
            [
                [
                    (
                        lambda a=a, b=b, ty=ty, tx=tx, dt=dt: weights_of(dt, a, b, ty, tx),
                        [
                            (
                                accs[a][2 * b + f],
                                lambda f=f, a=a, b=b, ty=ty, tx=tx, dt=dt: two_ref[
                                    b + tx, dt + f, a + ty : a + ty + 8
                                ].reshape(128, CH),
                            )
                            for f in range(2)
                        ],
                    )
                    for ty in range(2)
                    for tx in range(2)
                    for dt in range(3)
                ]
                for a in range(2)
            ]
        )
    for b in range(2):
        for a in range(2):
            for f in range(2):
                total = pltpu.matmul_pop(accs[a][2 * b + f]).reshape(8, 16, CH)
                for y in range(8):
                    value = silu(total[y] + second_bias)
                    value = jnp.where(own_rows[f] > y, value, 0.0)
                    for k in range(2):
                        row = ((k * 2 + f) * 16 + 2 * y + a) * 16 + b
                        for side in range(2):
                            mixed_ref[side, pl.ds(row, 8, stride=2), :] = value[
                                k * 8 : k * 8 + 8, side * 128 : side * 128 + 128
                            ]
    for side in range(2):
        out_ref[:, side * 128 : side * 128 + 128] = mixed_ref[side].astype(BF16)


def main_kernel(*refs):
    pl.run_scoped(
        functools.partial(main_body, *refs),
        *[pltpu.ACC(m)((128, CH), F32) for m in range(2) for _ in range(4)],
        *[pltpu.ACC(m)((32, CH), F32) for m in range(2)],
    )


def held(value):
    return pltpu.with_memory_space_constraint(value, pltpu.VMEM)


def vmem_spec():
    return pl.BlockSpec(memory_space=pltpu.VMEM)


def hbm_spec():
    return pl.BlockSpec(memory_space=pl.ANY)


def constants(sent, stem_weight, first):
    return pl.pallas_call(
        constants_kernel,
        out_shape=(
            pltpu.VMEM((512, 512), BF16),
            pltpu.VMEM((256, 768), BF16),
            pltpu.VMEM((3, 256, CH), BF16),
            pltpu.VMEM((EARLY, CH, CH), BF16),
        ),
        in_specs=[hbm_spec(), vmem_spec(), hbm_spec()],
        out_specs=(vmem_spec(),) * 4,
        scratch_shapes=[pltpu.SemaphoreType.DMA],
        compiler_params=pltpu.CompilerParams(vmem_limit_bytes=VMEM_LIMIT),
    )(sent, stem_weight.reshape(9, 48, CH), first)


def decode(
    tokens,
    place,
    lanes,
    spread,
    stem,
    stem_bias,
    ready,
    first,
    first_bias,
    second,
    second_bias,
):
    return pl.pallas_call(
        main_kernel,
        out_shape=jax.ShapeDtypeStruct((1024, CH), BF16),
        in_specs=[vmem_spec()] * 7 + [hbm_spec(), vmem_spec()] * 2,
        out_specs=vmem_spec(),
        scratch_shapes=[
            pltpu.VMEM((128, 128), F32),
            pltpu.VMEM((6, 10, 16, CH), BF16),
            pltpu.VMEM((3, 6, 10, 16, CH), BF16),
            pltpu.VMEM((3, 4, 10, 16, CH), BF16),
            pltpu.VMEM((27 - EARLY, CH, CH), BF16),
            pltpu.VMEM((3, 3, 3, CH, CH), BF16),
            pltpu.VMEM((3, 12, CH, CH), BF16),
            pltpu.VMEM((2, 1024, 128), F32),
            pltpu.SemaphoreType.DMA((4,)),
        ],
        compiler_params=pltpu.CompilerParams(vmem_limit_bytes=VMEM_LIMIT),
    )(
        tokens,
        place,
        lanes,
        spread,
        stem,
        stem_bias[None],
        ready,
        first,
        first_bias[None],
        second,
        second_bias[None],
    )


def body(
    transformer_tokens,
    frames,
    heights,
    widths,
    tile_decode_device,
    tile_device_slot,
    stem_conv_weight,
    stem_conv_bias,
    upsample_first_weight,
    upsample_first_bias,
    upsample_second_weight,
    upsample_second_bias,
):
    requests = lax.axis_size("req")
    half = requests // 2
    own = jnp.transpose(transformer_tokens[0, :, 0, :])
    other = lax.ppermute(own, "req", [(i, (i + half) % requests) for i in range(requests)])
    shape = jax.ShapeDtypeStruct
    params = pltpu.CompilerParams(vmem_limit_bytes=60 * 1024 * 1024)
    pick, place = pl.pallas_call(
        plan_kernel,
        out_shape=(
            pltpu.VMEM((256, 256), BF16),
            pltpu.VMEM((448, 128), BF16),
        ),
        in_specs=[vmem_spec()] * 5,
        out_specs=(vmem_spec(),) * 2,
        compiler_params=params,
    )(
        frames[None],
        heights[None],
        widths[None],
        jnp.transpose(tile_decode_device, (2, 1, 0)),
        jnp.transpose(tile_device_slot, (2, 1, 0)),
    )
    first = upsample_first_weight.reshape(27, CH, CH)
    sent = pl.pallas_call(
        pick_kernel,
        out_shape=pltpu.VMEM((SEQ, 8, 128), BF16),
        in_specs=[vmem_spec()] * 3,
        out_specs=vmem_spec(),
        scratch_shapes=[pltpu.VMEM((128, 128), F32)],
        compiler_params=pltpu.CompilerParams(vmem_limit_bytes=VMEM_LIMIT),
    )(held(own), held(other), held(pick))
    tokens = lax.all_to_all(sent, "seq", 0, 0, tiled=True)
    lanes, spread, stem, ready = constants(sent, stem_conv_weight, first)
    decoded = decode(
        held(tokens),
        held(place),
        held(lanes),
        held(spread),
        held(stem),
        stem_conv_bias,
        held(ready),
        first,
        upsample_first_bias,
        upsample_second_weight,
        upsample_second_bias,
    )
    return decoded.reshape(1, 1, 2, 2, 16, 16, CH)


def solution(mesh):
    placed = (P("req", None, "seq", None), P(), P(), P(), P(), P(), P(), P(), P(), P(), P(), P())
    return jax.shard_map(
        body,
        mesh=mesh,
        in_specs=placed,
        out_specs=P("req", "seq", None, None, None, None, None),
        check_vma=False,
    )
```

```python
import functools

import jax
import jax.numpy as jnp
from jax import lax
from jax.experimental import pallas as pl
from jax.experimental.pallas import tpu as pltpu
from jax.sharding import PartitionSpec as P

F32 = jnp.float32
BF16 = jnp.bfloat16
I32 = jnp.int32
CH = 256
SEQ = 16
TILES = 3
EARLY = 15
VMEM_LIMIT = 52 * 1024 * 1024


def iota(shape, dim):
    return lax.broadcasted_iota(I32, shape, dim)


def one(mask):
    return jnp.where(mask, 1.0, 0.0).astype(BF16)


def plan_kernel(
    frames_ref,
    heights_ref,
    widths_ref,
    device_ref,
    slot_ref,
    own_ref,
    pick_ref,
    base_ref,
    place_ref,
):
    me = lax.axis_index("req")
    column = lax.axis_index("seq")
    half = frames_ref.shape[1] // 2
    partner = lax.rem(me + half, 2 * half)

    lane = iota((1, 32), 1)

    def entry(ref, who):
        return jnp.sum(jnp.where(lane == who, ref[...], 0), axis=1, keepdims=True)

    dest = iota((SEQ, 1), 0)
    tile_lane = iota((SEQ, 32), 1)

    def of_request(ref, tile, who):
        return jnp.sum(jnp.where(tile_lane == who, ref[tile], 0), axis=1, keepdims=True)

    codes = []
    lims = []
    tops = []
    for k in range(2):
        code = jnp.zeros((SEQ, 1), I32)
        live = jnp.zeros((SEQ, 1), I32)
        taken = jnp.zeros((SEQ, 1), I32)
        for i in range(TILES):
            start = 32 * i + 2 * dest - 6
            for who, offset in ((me, 0), (partner, 128)):
                hit = (of_request(device_ref, i, who) == me) & (
                    of_request(slot_ref, i, who) == k
                )
                code = code + jnp.where(hit, start + offset, 0)
                live = live + jnp.where(hit, 1, 0)
                if offset:
                    taken = taken + jnp.where(hit, 1, 0)
        lim = jnp.where(
            taken > 0,
            128 + entry(frames_ref, partner),
            jnp.where(live > 0, entry(frames_ref, me), 0),
        )
        code = jnp.where(live > 0, code, -64)
        codes.append(code)
        lims.append(lim)
        mine = dest == column

        def at_mine(v, mine=mine):
            return jnp.sum(jnp.where(mine, v, 0), axis=0, keepdims=True)

        my_taken = at_mine(taken) > 0
        my_live = at_mine(live) > 0
        tops.append(
            (
                jnp.where(my_taken, entry(heights_ref, partner), entry(heights_ref, me)),
                jnp.where(my_taken, entry(widths_ref, partner), entry(widths_ref, me)),
                at_mine(code) - jnp.where(my_taken, 128, 0),
                jnp.where(
                    my_live,
                    jnp.where(my_taken, entry(frames_ref, partner), entry(frames_ref, me)),
                    -64,
                ),
            )
        )

    source = iota((SEQ, 128), 1)
    mine_rows = []
    for h in range(2):
        for k in range(2):
            for pair in range(4):
                row = (h * 8 + k * 4 + pair) * SEQ
                wanted = codes[k] + (2 * pair + h)
                mine_rows.append(one((source == wanted) & (source < lims[k])))
                pick_ref[row : row + SEQ, :] = one(
                    (source + 128 == wanted) & (source + 128 < lims[k])
                )
    mine_rows = jnp.concatenate(mine_rows, axis=0)
    base_ref[...] = picked(mine_rows[:, : own_ref.shape[1]], own_ref[...])

    second_slot = iota((16, 128), 0) >= 8
    for n in range(4):
        place_ref[384 + 16 * n : 400 + 16 * n, :] = (
            jnp.where(second_slot, tops[1][n], tops[0][n]).astype(F32).astype(BF16)
        )

    row = iota((384, 128), 0)
    col = iota((384, 128), 1)
    tap = row >> 7
    y = (row >> 4) & 7
    which = (row >> 3) & 1
    x = (row & 7) + tap - 1
    tall = jnp.where(which == 1, tops[1][0], tops[0][0])
    wide = jnp.where(which == 1, tops[1][1], tops[0][1])
    wanted = ((y & 1) * 2 + (x & 1)) * 32 + which * 16 + (y >> 1) * 4 + (x >> 1)
    place_ref[:384, :] = one((col == wanted) & (y < tall) & (x >= 0) & (x < wide))


def constants_kernel(
    sent_hbm,
    stem_ref,
    first_hbm,
    stem_bias_ref,
    first_bias_ref,
    second_bias_ref,
    lanes_ref,
    spread_ref,
    stem_out_ref,
    ready_ref,
    biases_ref,
    sem,
):
    early = pltpu.make_async_copy(first_hbm.at[:EARLY], ready_ref, sem)
    early.start()
    for n, ref in enumerate((stem_bias_ref, first_bias_ref, second_bias_ref)):
        biases_ref[n] = jnp.broadcast_to(ref[...], (8, CH))
    row = iota((512, 512), 0)
    col = iota((512, 512), 1)
    lanes_ref[...] = one(col == (row & 3) * 128 + (row >> 6) * 16 + ((row >> 2) & 15))

    row = iota((256, 768), 0)
    col = iota((256, 768), 1)
    step = (col >> 4) & 3
    spread_ref[...] = one(
        (row >> 7 == (col >> 6) & 1)
        & (step < 3)
        & ((row >> 4) & 7 == (col >> 7) + step)
        & (row & 15 == col & 15)
    )

    stem_out_ref[...] = jnp.zeros(stem_out_ref.shape, BF16)
    for dy in range(3):
        for dx in range(3):
            stem_out_ref[dy, dx * 64 : dx * 64 + 48, :] = stem_ref[dy * 3 + dx]
    early.wait()


def picked(pick, tokens):
    rows = lax.dot_general(pick, tokens, (((1,), (1,)), ((), ())), preferred_element_type=F32)
    return jnp.concatenate([rows[:128], rows[128:]], axis=1)


def pick_kernel(other_ref, pick_ref, base_ref, out_ref, rows_ref):
    joined = base_ref[...] + picked(pick_ref[:, : other_ref.shape[1]], other_ref[...])
    for part in range(8):
        rows_ref[pl.ds(part, SEQ, stride=8), :] = joined[part * SEQ : (part + 1) * SEQ]
    out_ref[...] = rows_ref[...].astype(BF16).reshape(out_ref.shape)


def silu(v):
    halved = 0.5 * v
    return halved + halved * jnp.tanh(halved)


def store_taps(ref, frame, y, value):
    split = value.reshape(2, 8, CH)
    column = iota((2, 8, CH), 1)
    before = jnp.where(column == 0, 0.0, pltpu.roll(split, 1, 1))
    after = jnp.where(column == 7, 0.0, pltpu.roll(split, 7, 1))
    ref[0, frame, y + 1] = before.reshape(16, CH).astype(BF16)
    ref[1, frame, y + 1] = value.astype(BF16)
    ref[2, frame, y + 1] = after.reshape(16, CH).astype(BF16)


def multiply(work, beside=()):
    for m, steps in enumerate(work):
        pltpu.matmul_push_rhs(steps[0][0](), 0, m)
    for n in range(max(len(steps) for steps in work)):
        for m, steps in enumerate(work):
            if n + 1 < len(steps):
                pltpu.matmul_push_rhs(steps[n + 1][0](), (n + 1) % 2, m)
            if n < len(steps):
                for order, (acc, rows) in enumerate(steps[n][1]):
                    pltpu.matmul_acc_lhs(acc, rows(), load_staged_rhs=n % 2 if order == 0 else None)
        for step, thunk in beside:
            if step == n:
                thunk()


def main_body(
    tokens_ref,
    place_ref,
    lanes_ref,
    spread_ref,
    stem_ref,
    ready_ref,
    biases_ref,
    first_hbm,
    second_hbm,
    out_hbm,
    rows_ref,
    taps_ref,
    one_ref,
    two_ref,
    first_ref,
    second_ref,
    folded_ref,
    mixed_ref,
    stage_ref,
    sems,
    *accs,
):
    accs, small = (accs[:4], accs[4:8]), accs[8:]
    copies = [pltpu.make_async_copy(first_hbm.at[EARLY:], first_ref, sems.at[3])]
    fetches = [
        pltpu.make_async_copy(second_hbm.at[:, :, t], second_ref.at[t], sems.at[t]) for t in range(3)
    ]
    for copy in copies + fetches:
        copy.start()

    rows_ref[...] = tokens_ref[...].reshape(128, 128).astype(F32)
    window = jnp.concatenate(
        [
            jnp.concatenate(
                [rows_ref[pl.ds(k * 4 + pair, SEQ, stride=8), :] for pair in range(4)], axis=1
            )
            for k in range(2)
        ],
        axis=0,
    ).astype(BF16)
    multiply(
        [
            [
                (
                    lambda m=m, k=k: lanes_ref[k * CH : k * CH + CH, m * CH : m * CH + CH],
                    [(small[m], lambda k=k: window[:, k * CH : k * CH + CH])],
                )
                for k in range(2)
            ]
            for m in range(2)
        ]
    )
    parity = [pltpu.matmul_pop(small[m]).astype(BF16) for m in range(2)]
    blank = jnp.zeros((128, 128), BF16)
    stacked = jnp.concatenate(
        [parity[n // 2][:, n % 2 * 128 : n % 2 * 128 + 128] for n in range(4)], axis=0
    )
    stacked = jnp.concatenate(
        [jnp.concatenate([stacked, blank], axis=1), jnp.zeros((128, CH), BF16)], axis=0
    )
    multiply(
        [
            [
                (
                    lambda: stacked,
                    [
                        (
                            accs[m][n],
                            lambda t=2 * m + n: jnp.concatenate(
                                [place_ref[t * 128 : t * 128 + 128], blank], axis=1
                            ),
                        )
                        for n in range(2 - m)
                    ],
                )
            ]
            for m in range(2)
        ]
    )
    placed = [
        pltpu.matmul_pop(acc)[:, :128].astype(BF16) for acc in (accs[0][0], accs[0][1], accs[1][0])
    ]
    joined = (
        jnp.concatenate(placed[:2], axis=1),
        jnp.concatenate([placed[2], blank], axis=1),
    )
    multiply(
        [
            [
                (
                    lambda t=t: spread_ref[:, t * CH : t * CH + CH],
                    [(accs[m][t // 2 * 2 + n], lambda n=n: joined[n]) for n in range(2)],
                )
                for t in range(m, 3, 2)
            ]
            for m in range(2)
        ]
    )
    spread_out = [
        [pltpu.matmul_pop(accs[t % 2][t // 2 * 2 + n]).astype(BF16) for n in range(2)] for t in range(3)
    ]
    zero_row = jnp.zeros((16, CH), BF16)
    for g in range(6):
        lanes = slice(g % 2 * 128, g % 2 * 128 + 128)
        near, far = spread_out[g // 2]
        taps_ref[g, 0] = zero_row
        taps_ref[g, 1:9, :, :128] = near[:, lanes].reshape(8, 16, 128)
        taps_ref[g, 1:9, :, 128:] = far[:, lanes].reshape(8, 16, 128)
        taps_ref[g, 9] = zero_row
        for dx in range(3):
            one_ref[dx, g, 0] = zero_row
            one_ref[dx, g, 9] = zero_row
    for g in range(4):
        for dx in range(3):
            two_ref[dx, g, 0] = zero_row
            two_ref[dx, g, 9] = zero_row

    tall, wide, start, count = (
        place_ref[384 + 16 * n : 400 + 16 * n, :].astype(F32).astype(I32) for n in range(4)
    )
    tall = jnp.where((iota((16, 128), 0) & 7) < wide, tall, 0)

    def limit(keep):
        rows = jnp.where(keep, tall, 0)
        return jnp.concatenate([rows, rows], axis=1)

    def finish(frame, rows, y, total, bias, ref):
        store_taps(ref, frame, y, jnp.where(rows > y, silu(total + bias), 0.0))

    stem_bias = biases_ref[0, 0:1]
    multiply(
        [
            [
                (
                    lambda dy=dy: stem_ref[dy],
                    [
                        (accs[m][n], lambda g=3 * m + n, dy=dy: taps_ref[g, dy : dy + 8].reshape(128, CH))
                        for n in range(3)
                    ],
                )
                for dy in range(3)
            ]
            for m in range(2)
        ]
    )
    for n in range(3):
        for m in range(2):
            hidden = pltpu.matmul_pop(accs[m][n]).reshape(8, 16, CH)
            rows = limit(start + (2 + 3 * m + n) >= 0)
            for y in range(8):
                finish(3 * m + n, rows, y, hidden[y], stem_bias, one_ref)

    first_bias = biases_ref[1, 0:1]
    taps = [(dy, dx, dt) for dy in range(3) for dx in range(3) for dt in range(3)]
    corners = {(0, 0, 0, 0): (0, 0), (0, 1, 0, 1): (0, 2), (1, 0, 1, 0): (2, 0), (1, 1, 1, 1): (2, 2)}
    sums = [
        key
        for key in ((a, b, ty, tx) for a in range(2) for b in range(2) for ty in range(2) for tx in range(2))
        if key not in corners
    ]

    def fold(t):
        fetches[t].wait()
        for part in range(0, CH, 64):
            rows = slice(part, part + 64)
            w = [[second_ref[t, u, v, rows, :] for v in range(3)] for u in range(3)]
            by_row = [
                (w[0][v], w[1][v] + w[2][v], w[0][v] + w[1][v], w[2][v]) for v in range(3)
            ]
            for place, (a, b, ty, tx) in enumerate(sums):
                c = [by_row[v][2 * a + ty] for v in range(3)]
                folded_ref[t, place, rows, :] = (c[0], c[1] + c[2], c[0] + c[1], c[2])[2 * b + tx]

    def weights_of(t, *key):
        if key in corners:
            return second_ref[(t,) + corners[key]]
        return folded_ref[t, sums.index(key)]

    def first_weights(tap):
        place = tap[0] * 9 + tap[1] * 3 + tap[2]
        if place == EARLY:
            copies[0].wait()
        return ready_ref[place] if place < EARLY else first_ref[place - EARLY]

    multiply(
        [
            [
                (
                    lambda tap=tap: first_weights(tap),
                    [
                        (
                            accs[m][n],
                            lambda n=n, tap=tap: one_ref[
                                tap[1], tap[2] + n, tap[0] : tap[0] + 8
                            ].reshape(128, CH),
                        )
                        for n in range(4)
                    ],
                )
                for tap in taps[m::2]
            ]
            for m in range(2)
        ],
    )
    for t in range(3):
        fold(t)
    for g in range(4):
        total = pltpu.matmul_pop(accs[0][g]) + pltpu.matmul_pop(accs[1][g])
        total = total.reshape(8, 16, CH)
        rows = limit(start + (4 + g) >= 0)
        for y in range(8):
            finish(g, rows, y, total[y], first_bias, two_ref)

    second_bias = biases_ref[2, 0:1]
    own_rows = [limit(start + (6 + f) < count) for f in range(2)]
    for b in range(2):
        multiply(
            [
                [
                    (
                        lambda a=a, b=b, ty=ty, tx=tx, dt=dt: weights_of(dt, a, b, ty, tx),
                        [
                            (
                                accs[a][2 * b + f],
                                lambda f=f, a=a, b=b, ty=ty, tx=tx, dt=dt: two_ref[
                                    b + tx, dt + f, a + ty : a + ty + 8
                                ].reshape(128, CH),
                            )
                            for f in range(2)
                        ],
                    )
                    for ty in range(2)
                    for tx in range(2)
                    for dt in range(3)
                ]
                for a in range(2)
            ]
        )
    sends = []
    for f in range(2):
        for b in range(2):
            for a in range(2):
                total = pltpu.matmul_pop(accs[a][2 * b + f]).reshape(8, 16, CH)
                for y in range(8):
                    value = silu(total[y] + second_bias)
                    value = jnp.where(own_rows[f] > y, value, 0.0)
                    for k in range(2):
                        row = ((k * 2 + f) * 16 + 2 * y + a) * 16 + b
                        for side in range(2):
                            mixed_ref[side, pl.ds(row, 8, stride=2), :] = value[
                                k * 8 : k * 8 + 8, side * 128 : side * 128 + 128
                            ]
        for k in range(2):
            rows = slice((k * 2 + f) * 256, (k * 2 + f) * 256 + 256)
            for side in range(2):
                stage_ref[k, f, :, side * 128 : side * 128 + 128] = mixed_ref[side, rows].astype(BF16)
            send = pltpu.make_async_copy(stage_ref.at[k, f], out_hbm.at[k, f], sems.at[4 + 2 * f + k])
            send.start()
            sends.append(send)
    for send in sends:
        send.wait()


def main_kernel(*refs):
    pl.run_scoped(
        functools.partial(main_body, *refs),
        *[pltpu.ACC(m)((128, CH), F32) for m in range(2) for _ in range(4)],
        *[pltpu.ACC(m)((32, CH), F32) for m in range(2)],
    )


def held(value):
    return pltpu.with_memory_space_constraint(value, pltpu.VMEM)


def vmem_spec():
    return pl.BlockSpec(memory_space=pltpu.VMEM)


def hbm_spec():
    return pl.BlockSpec(memory_space=pl.ANY)


def constants(sent, stem_weight, first, biases):
    return pl.pallas_call(
        constants_kernel,
        out_shape=(
            pltpu.VMEM((512, 512), BF16),
            pltpu.VMEM((256, 768), BF16),
            pltpu.VMEM((3, 256, CH), BF16),
            pltpu.VMEM((EARLY, CH, CH), BF16),
            pltpu.VMEM((3, 8, CH), F32),
        ),
        in_specs=[hbm_spec(), vmem_spec(), hbm_spec()] + [vmem_spec()] * 3,
        out_specs=(vmem_spec(),) * 5,
        scratch_shapes=[pltpu.SemaphoreType.DMA],
        compiler_params=pltpu.CompilerParams(vmem_limit_bytes=VMEM_LIMIT),
    )(sent, stem_weight.reshape(9, 48, CH), first, *(bias[None] for bias in biases))


def decode(
    tokens,
    place,
    lanes,
    spread,
    stem,
    ready,
    biases,
    first,
    second,
):
    return pl.pallas_call(
        main_kernel,
        out_shape=jax.ShapeDtypeStruct((2, 2, 256, CH), BF16),
        in_specs=[vmem_spec()] * 7 + [hbm_spec()] * 2,
        out_specs=hbm_spec(),
        scratch_shapes=[
            pltpu.VMEM((128, 128), F32),
            pltpu.VMEM((6, 10, 16, CH), BF16),
            pltpu.VMEM((3, 6, 10, 16, CH), BF16),
            pltpu.VMEM((3, 4, 10, 16, CH), BF16),
            pltpu.VMEM((27 - EARLY, CH, CH), BF16),
            pltpu.VMEM((3, 3, 3, CH, CH), BF16),
            pltpu.VMEM((3, 12, CH, CH), BF16),
            pltpu.VMEM((2, 1024, 128), F32),
            pltpu.VMEM((2, 2, 256, CH), BF16),
            pltpu.SemaphoreType.DMA((8,)),
        ],
        compiler_params=pltpu.CompilerParams(vmem_limit_bytes=VMEM_LIMIT),
    )(
        tokens,
        place,
        lanes,
        spread,
        stem,
        ready,
        biases,
        first,
        second,
    )


def body(
    transformer_tokens,
    frames,
    heights,
    widths,
    tile_decode_device,
    tile_device_slot,
    stem_conv_weight,
    stem_conv_bias,
    upsample_first_weight,
    upsample_first_bias,
    upsample_second_weight,
    upsample_second_bias,
):
    requests = lax.axis_size("req")
    half = requests // 2
    own = jnp.transpose(transformer_tokens[0, :, 0, :])
    other = lax.ppermute(own, "req", [(i, (i + half) % requests) for i in range(requests)])
    shape = jax.ShapeDtypeStruct
    params = pltpu.CompilerParams(vmem_limit_bytes=60 * 1024 * 1024)
    pick, base, place = pl.pallas_call(
        plan_kernel,
        out_shape=(
            pltpu.VMEM((256, 128), BF16),
            pltpu.VMEM((128, 128), F32),
            pltpu.VMEM((448, 128), BF16),
        ),
        in_specs=[vmem_spec()] * 6,
        out_specs=(vmem_spec(),) * 3,
        compiler_params=params,
    )(
        frames[None],
        heights[None],
        widths[None],
        jnp.transpose(tile_decode_device, (2, 1, 0)),
        jnp.transpose(tile_device_slot, (2, 1, 0)),
        own,
    )
    first = upsample_first_weight.reshape(27, CH, CH)
    sent = pl.pallas_call(
        pick_kernel,
        out_shape=pltpu.VMEM((SEQ, 8, 128), BF16),
        in_specs=[vmem_spec()] * 3,
        out_specs=vmem_spec(),
        scratch_shapes=[pltpu.VMEM((128, 128), F32)],
        compiler_params=pltpu.CompilerParams(vmem_limit_bytes=VMEM_LIMIT),
    )(held(other), held(pick), held(base))
    tokens = lax.all_to_all(sent, "seq", 0, 0, tiled=True)
    lanes, spread, stem, ready, biases = constants(
        sent, stem_conv_weight, first, (stem_conv_bias, upsample_first_bias, upsample_second_bias)
    )
    decoded = decode(
        held(tokens),
        held(place),
        held(lanes),
        held(spread),
        held(stem),
        held(ready),
        held(biases),
        first,
        upsample_second_weight,
    )
    return decoded.reshape(1, 1, 2, 2, 16, 16, CH)


def solution(mesh):
    placed = (P("req", None, "seq", None), P(), P(), P(), P(), P(), P(), P(), P(), P(), P(), P())
    return jax.shard_map(
        body,
        mesh=mesh,
        in_specs=placed,
        out_specs=P("req", "seq", None, None, None, None, None),
        check_vma=False,
    )
```

```python
import functools

import jax
import jax.numpy as jnp
from jax import lax
from jax.experimental import pallas as pl
from jax.experimental.pallas import tpu as pltpu
from jax.sharding import PartitionSpec as P

F32 = jnp.float32
BF16 = jnp.bfloat16
I32 = jnp.int32
CH = 256
SEQ = 16
TILES = 3
EARLY = 15
VMEM_LIMIT = 52 * 1024 * 1024


def iota(shape, dim):
    return lax.broadcasted_iota(I32, shape, dim)


def one(mask):
    return jnp.where(mask, 1.0, 0.0).astype(BF16)


def plan_kernel(
    frames_ref,
    heights_ref,
    widths_ref,
    device_ref,
    slot_ref,
    own_ref,
    pick_ref,
    base_ref,
    place_ref,
    rows_ref,
):
    me = lax.axis_index("req")
    column = lax.axis_index("seq")
    half = frames_ref.shape[1] // 2
    partner = lax.rem(me + half, 2 * half)

    lane = iota((1, 32), 1)

    def entry(ref, who):
        return jnp.sum(jnp.where(lane == who, ref[...], 0), axis=1, keepdims=True)

    dest = iota((SEQ, 1), 0)
    tile_lane = iota((SEQ, 32), 1)

    def of_request(ref, tile, who):
        return jnp.sum(jnp.where(tile_lane == who, ref[tile], 0), axis=1, keepdims=True)

    codes = []
    lims = []
    tops = []
    for k in range(2):
        code = jnp.zeros((SEQ, 1), I32)
        live = jnp.zeros((SEQ, 1), I32)
        taken = jnp.zeros((SEQ, 1), I32)
        for i in range(TILES):
            start = 32 * i + 2 * dest - 6
            for who, offset in ((me, 0), (partner, 128)):
                hit = (of_request(device_ref, i, who) == me) & (
                    of_request(slot_ref, i, who) == k
                )
                code = code + jnp.where(hit, start + offset, 0)
                live = live + jnp.where(hit, 1, 0)
                if offset:
                    taken = taken + jnp.where(hit, 1, 0)
        lim = jnp.where(
            taken > 0,
            128 + entry(frames_ref, partner),
            jnp.where(live > 0, entry(frames_ref, me), 0),
        )
        code = jnp.where(live > 0, code, -64)
        codes.append(code)
        lims.append(lim)
        mine = dest == column

        def at_mine(v, mine=mine):
            return jnp.sum(jnp.where(mine, v, 0), axis=0, keepdims=True)

        my_taken = at_mine(taken) > 0
        my_live = at_mine(live) > 0
        tops.append(
            (
                jnp.where(my_taken, entry(heights_ref, partner), entry(heights_ref, me)),
                jnp.where(my_taken, entry(widths_ref, partner), entry(widths_ref, me)),
                at_mine(code) - jnp.where(my_taken, 128, 0),
                jnp.where(
                    my_live,
                    jnp.where(my_taken, entry(frames_ref, partner), entry(frames_ref, me)),
                    -64,
                ),
            )
        )

    source = iota((SEQ, 128), 1)
    for h in range(2):
        for k in range(2):
            for pair in range(4):
                wanted = codes[k] + (2 * pair + h)
                rows = pl.ds(h * 128 + k * 4 + pair, SEQ, stride=8)
                mine = (source == wanted) & (source < lims[k])
                theirs = (source + 128 == wanted) & (source + 128 < lims[k])
                rows_ref[0, rows, :] = jnp.where(mine, 1.0, 0.0)
                rows_ref[1, rows, :] = jnp.where(theirs, 1.0, 0.0)
    pick_ref[...] = rows_ref[1].astype(BF16)
    base_ref[...] = picked(rows_ref[0, :, : own_ref.shape[1]].astype(BF16), own_ref[...])

    second_slot = iota((16, 128), 0) >= 8
    for n in range(4):
        place_ref[384 + 16 * n : 400 + 16 * n, :] = (
            jnp.where(second_slot, tops[1][n], tops[0][n]).astype(F32).astype(BF16)
        )

    row = iota((384, 128), 0)
    col = iota((384, 128), 1)
    tap = row >> 7
    y = (row >> 4) & 7
    which = (row >> 3) & 1
    x = (row & 7) + tap - 1
    tall = jnp.where(which == 1, tops[1][0], tops[0][0])
    wide = jnp.where(which == 1, tops[1][1], tops[0][1])
    wanted = ((y & 1) * 2 + (x & 1)) * 32 + which * 16 + (y >> 1) * 4 + (x >> 1)
    place_ref[:384, :] = one((col == wanted) & (y < tall) & (x >= 0) & (x < wide))


def constants_kernel(
    sent_hbm,
    stem_ref,
    first_hbm,
    stem_bias_ref,
    first_bias_ref,
    second_bias_ref,
    lanes_ref,
    spread_ref,
    stem_out_ref,
    ready_ref,
    biases_ref,
    sem,
):
    early = pltpu.make_async_copy(first_hbm.at[:EARLY], ready_ref, sem)
    early.start()
    for n, ref in enumerate((stem_bias_ref, first_bias_ref, second_bias_ref)):
        biases_ref[n] = jnp.broadcast_to(ref[...], (8, CH))
    row = iota((512, 512), 0)
    col = iota((512, 512), 1)
    lanes_ref[...] = one(col == (row & 3) * 128 + (row >> 6) * 16 + ((row >> 2) & 15))

    row = iota((256, 768), 0)
    col = iota((256, 768), 1)
    step = (col >> 4) & 3
    spread_ref[...] = one(
        (row >> 7 == (col >> 6) & 1)
        & (step < 3)
        & ((row >> 4) & 7 == (col >> 7) + step)
        & (row & 15 == col & 15)
    )

    stem_out_ref[...] = jnp.zeros(stem_out_ref.shape, BF16)
    for dy in range(3):
        for dx in range(3):
            stem_out_ref[dy, dx * 64 : dx * 64 + 48, :] = stem_ref[dy * 3 + dx]
    early.wait()


def picked(pick, tokens):
    rows = lax.dot_general(pick, tokens, (((1,), (1,)), ((), ())), preferred_element_type=F32)
    return jnp.concatenate([rows[:128], rows[128:]], axis=1)


def pick_kernel(other_ref, pick_ref, base_ref, out_ref):
    joined = base_ref[...] + picked(pick_ref[:, : other_ref.shape[1]], other_ref[...])
    out_ref[...] = joined.astype(BF16).reshape(out_ref.shape)


def silu(v):
    halved = 0.5 * v
    return halved + halved * jnp.tanh(halved)


def store_taps(ref, frame, y, value):
    split = value.reshape(2, 8, CH)
    column = iota((2, 8, CH), 1)
    before = jnp.where(column == 0, 0.0, pltpu.roll(split, 1, 1))
    after = jnp.where(column == 7, 0.0, pltpu.roll(split, 7, 1))
    ref[0, frame, y + 1] = before.reshape(16, CH).astype(BF16)
    ref[1, frame, y + 1] = value.astype(BF16)
    ref[2, frame, y + 1] = after.reshape(16, CH).astype(BF16)


def multiply(work, beside=()):
    for m, steps in enumerate(work):
        pltpu.matmul_push_rhs(steps[0][0](), 0, m)
    for n in range(max(len(steps) for steps in work)):
        for m, steps in enumerate(work):
            if n + 1 < len(steps):
                pltpu.matmul_push_rhs(steps[n + 1][0](), (n + 1) % 2, m)
            if n < len(steps):
                for order, (acc, rows) in enumerate(steps[n][1]):
                    pltpu.matmul_acc_lhs(acc, rows(), load_staged_rhs=n % 2 if order == 0 else None)
        for step, thunk in beside:
            if step == n:
                thunk()


def main_body(
    tokens_ref,
    place_ref,
    lanes_ref,
    spread_ref,
    stem_ref,
    ready_ref,
    biases_ref,
    first_hbm,
    second_hbm,
    out_hbm,
    rows_ref,
    taps_ref,
    one_ref,
    two_ref,
    first_ref,
    second_ref,
    folded_ref,
    mixed_ref,
    stage_ref,
    sems,
    *accs,
):
    accs, small = (accs[:4], accs[4:8]), accs[8:]
    copies = [pltpu.make_async_copy(first_hbm.at[EARLY:], first_ref, sems.at[3])]
    fetches = [
        pltpu.make_async_copy(second_hbm.at[:, :, t], second_ref.at[t], sems.at[t]) for t in range(3)
    ]
    for copy in copies + fetches:
        copy.start()

    rows_ref[...] = tokens_ref[...].reshape(128, 128).astype(F32)
    window = jnp.concatenate(
        [
            jnp.concatenate(
                [rows_ref[pl.ds(k * 4 + pair, SEQ, stride=8), :] for pair in range(4)], axis=1
            )
            for k in range(2)
        ],
        axis=0,
    ).astype(BF16)
    multiply(
        [
            [
                (
                    lambda m=m, k=k: lanes_ref[k * CH : k * CH + CH, m * CH : m * CH + CH],
                    [(small[m], lambda k=k: window[:, k * CH : k * CH + CH])],
                )
                for k in range(2)
            ]
            for m in range(2)
        ]
    )
    parity = [pltpu.matmul_pop(small[m]).astype(BF16) for m in range(2)]
    blank = jnp.zeros((128, 128), BF16)
    stacked = jnp.concatenate(
        [parity[n // 2][:, n % 2 * 128 : n % 2 * 128 + 128] for n in range(4)], axis=0
    )
    stacked = jnp.concatenate(
        [jnp.concatenate([stacked, blank], axis=1), jnp.zeros((128, CH), BF16)], axis=0
    )
    multiply(
        [
            [
                (
                    lambda: stacked,
                    [
                        (
                            accs[m][n],
                            lambda t=2 * m + n: jnp.concatenate(
                                [place_ref[t * 128 : t * 128 + 128], blank], axis=1
                            ),
                        )
                        for n in range(2 - m)
                    ],
                )
            ]
            for m in range(2)
        ]
    )
    placed = [
        pltpu.matmul_pop(acc)[:, :128].astype(BF16) for acc in (accs[0][0], accs[0][1], accs[1][0])
    ]
    joined = (
        jnp.concatenate(placed[:2], axis=1),
        jnp.concatenate([placed[2], blank], axis=1),
    )
    multiply(
        [
            [
                (
                    lambda t=t: spread_ref[:, t * CH : t * CH + CH],
                    [(accs[m][t // 2 * 2 + n], lambda n=n: joined[n]) for n in range(2)],
                )
                for t in range(m, 3, 2)
            ]
            for m in range(2)
        ]
    )
    spread_out = [
        [pltpu.matmul_pop(accs[t % 2][t // 2 * 2 + n]).astype(BF16) for n in range(2)] for t in range(3)
    ]
    zero_row = jnp.zeros((16, CH), BF16)
    for g in range(6):
        lanes = slice(g % 2 * 128, g % 2 * 128 + 128)
        near, far = spread_out[g // 2]
        taps_ref[g, 0] = zero_row
        taps_ref[g, 1:9, :, :128] = near[:, lanes].reshape(8, 16, 128)
        taps_ref[g, 1:9, :, 128:] = far[:, lanes].reshape(8, 16, 128)
        taps_ref[g, 9] = zero_row
        for dx in range(3):
            one_ref[dx, g, 0] = zero_row
            one_ref[dx, g, 9] = zero_row
    for g in range(4):
        for dx in range(3):
            two_ref[dx, g, 0] = zero_row
            two_ref[dx, g, 9] = zero_row

    tall, wide, start, count = (
        place_ref[384 + 16 * n : 400 + 16 * n, :].astype(F32).astype(I32) for n in range(4)
    )
    tall = jnp.where((iota((16, 128), 0) & 7) < wide, tall, 0)

    def limit(keep):
        rows = jnp.where(keep, tall, 0)
        return jnp.concatenate([rows, rows], axis=1)

    def finish(frame, rows, y, total, bias, ref):
        store_taps(ref, frame, y, jnp.where(rows > y, silu(total + bias), 0.0))

    stem_bias = biases_ref[0, 0:1]
    multiply(
        [
            [
                (
                    lambda dy=dy: stem_ref[dy],
                    [
                        (accs[m][n], lambda g=3 * m + n, dy=dy: taps_ref[g, dy : dy + 8].reshape(128, CH))
                        for n in range(3)
                    ],
                )
                for dy in range(3)
            ]
            for m in range(2)
        ]
    )
    for n in range(3):
        for m in range(2):
            hidden = pltpu.matmul_pop(accs[m][n]).reshape(8, 16, CH)
            rows = limit(start + (2 + 3 * m + n) >= 0)
            for y in range(8):
                finish(3 * m + n, rows, y, hidden[y], stem_bias, one_ref)

    first_bias = biases_ref[1, 0:1]
    taps = [(dy, dx, dt) for dy in range(3) for dx in range(3) for dt in range(3)]
    corners = {(0, 0, 0, 0): (0, 0), (0, 1, 0, 1): (0, 2), (1, 0, 1, 0): (2, 0), (1, 1, 1, 1): (2, 2)}
    sums = [
        key
        for key in ((a, b, ty, tx) for a in range(2) for b in range(2) for ty in range(2) for tx in range(2))
        if key not in corners
    ]

    def fold(t):
        fetches[t].wait()
        for part in range(0, CH, 64):
            rows = slice(part, part + 64)
            w = [[second_ref[t, u, v, rows, :] for v in range(3)] for u in range(3)]
            by_row = [
                (w[0][v], w[1][v] + w[2][v], w[0][v] + w[1][v], w[2][v]) for v in range(3)
            ]
            for place, (a, b, ty, tx) in enumerate(sums):
                c = [by_row[v][2 * a + ty] for v in range(3)]
                folded_ref[t, place, rows, :] = (c[0], c[1] + c[2], c[0] + c[1], c[2])[2 * b + tx]

    def weights_of(t, *key):
        if key in corners:
            return second_ref[(t,) + corners[key]]
        return folded_ref[t, sums.index(key)]

    def first_weights(tap):
        place = tap[0] * 9 + tap[1] * 3 + tap[2]
        if place == EARLY:
            copies[0].wait()
        return ready_ref[place] if place < EARLY else first_ref[place - EARLY]

    multiply(
        [
            [
                (
                    lambda tap=tap: first_weights(tap),
                    [
                        (
                            accs[m][n],
                            lambda n=n, tap=tap: one_ref[
                                tap[1], tap[2] + n, tap[0] : tap[0] + 8
                            ].reshape(128, CH),
                        )
                        for n in range(4)
                    ],
                )
                for tap in taps[m::2]
            ]
            for m in range(2)
        ],
    )
    for t in range(3):
        fold(t)
    for g in range(4):
        total = pltpu.matmul_pop(accs[0][g]) + pltpu.matmul_pop(accs[1][g])
        total = total.reshape(8, 16, CH)
        rows = limit(start + (4 + g) >= 0)
        for y in range(8):
            finish(g, rows, y, total[y], first_bias, two_ref)

    second_bias = biases_ref[2, 0:1]
    own_rows = [limit(start + (6 + f) < count) for f in range(2)]
    def second_step(t, a, b, ty, tx):
        return (
            lambda: weights_of(t, a, b, ty, tx),
            [
                (
                    accs[a][2 * b + f],
                    lambda f=f: two_ref[b + tx, t + f, a + ty : a + ty + 8].reshape(128, CH),
                )
                for f in range(2)
            ],
        )

    values = {}

    def second_rows(a, b, f, rows):
        if (a, b, f) not in values:
            values[a, b, f] = pltpu.matmul_pop(accs[a][2 * b + f]).reshape(8, 16, CH)
        for y in rows:
            value = silu(values[a, b, f][y] + second_bias)
            value = jnp.where(own_rows[f] > y, value, 0.0)
            for k in range(2):
                row = ((k * 2 + f) * 16 + 2 * y + a) * 16 + b
                for side in range(2):
                    mixed_ref[side, pl.ds(row, 8, stride=2), :] = value[
                        k * 8 : k * 8 + 8, side * 128 : side * 128 + 128
                    ]

    taps = [(ty, tx) for ty in range(2) for tx in range(2)]
    multiply(
        [
            [second_step(t, a, b, *tap) for b in range(2) for t in range(3) for tap in taps]
            for a in range(2)
        ],
        [
            (14 + (f * 2 + a) * 2 + part, functools.partial(second_rows, a, 0, f, range(part * 4, part * 4 + 4)))
            for f in range(2)
            for a in range(2)
            for part in range(2)
        ],
    )
    sends = []
    for f in range(2):
        for a in range(2):
            second_rows(a, 1, f, range(8))
        for k in range(2):
            rows = slice((k * 2 + f) * 256, (k * 2 + f) * 256 + 256)
            for side in range(2):
                stage_ref[k, f, :, side * 128 : side * 128 + 128] = mixed_ref[side, rows].astype(BF16)
            send = pltpu.make_async_copy(stage_ref.at[k, f], out_hbm.at[k, f], sems.at[4 + 2 * f + k])
            send.start()
            sends.append(send)
    for send in sends:
        send.wait()


def main_kernel(*refs):
    pl.run_scoped(
        functools.partial(main_body, *refs),
        *[pltpu.ACC(m)((128, CH), F32) for m in range(2) for _ in range(4)],
        *[pltpu.ACC(m)((32, CH), F32) for m in range(2)],
    )


def held(value):
    return pltpu.with_memory_space_constraint(value, pltpu.VMEM)


def vmem_spec():
    return pl.BlockSpec(memory_space=pltpu.VMEM)


def hbm_spec():
    return pl.BlockSpec(memory_space=pl.ANY)


def constants(sent, stem_weight, first, biases):
    return pl.pallas_call(
        constants_kernel,
        out_shape=(
            pltpu.VMEM((512, 512), BF16),
            pltpu.VMEM((256, 768), BF16),
            pltpu.VMEM((3, 256, CH), BF16),
            pltpu.VMEM((EARLY, CH, CH), BF16),
            pltpu.VMEM((3, 8, CH), F32),
        ),
        in_specs=[hbm_spec(), vmem_spec(), hbm_spec()] + [vmem_spec()] * 3,
        out_specs=(vmem_spec(),) * 5,
        scratch_shapes=[pltpu.SemaphoreType.DMA],
        compiler_params=pltpu.CompilerParams(vmem_limit_bytes=VMEM_LIMIT),
    )(sent, stem_weight.reshape(9, 48, CH), first, *(bias[None] for bias in biases))


def decode(
    tokens,
    place,
    lanes,
    spread,
    stem,
    ready,
    biases,
    first,
    second,
):
    return pl.pallas_call(
        main_kernel,
        out_shape=jax.ShapeDtypeStruct((2, 2, 256, CH), BF16),
        in_specs=[vmem_spec()] * 7 + [hbm_spec()] * 2,
        out_specs=hbm_spec(),
        scratch_shapes=[
            pltpu.VMEM((128, 128), F32),
            pltpu.VMEM((6, 10, 16, CH), BF16),
            pltpu.VMEM((3, 6, 10, 16, CH), BF16),
            pltpu.VMEM((3, 4, 10, 16, CH), BF16),
            pltpu.VMEM((27 - EARLY, CH, CH), BF16),
            pltpu.VMEM((3, 3, 3, CH, CH), BF16),
            pltpu.VMEM((3, 12, CH, CH), BF16),
            pltpu.VMEM((2, 1024, 128), F32),
            pltpu.VMEM((2, 2, 256, CH), BF16),
            pltpu.SemaphoreType.DMA((8,)),
        ],
        compiler_params=pltpu.CompilerParams(vmem_limit_bytes=VMEM_LIMIT),
    )(
        tokens,
        place,
        lanes,
        spread,
        stem,
        ready,
        biases,
        first,
        second,
    )


def body(
    transformer_tokens,
    frames,
    heights,
    widths,
    tile_decode_device,
    tile_device_slot,
    stem_conv_weight,
    stem_conv_bias,
    upsample_first_weight,
    upsample_first_bias,
    upsample_second_weight,
    upsample_second_bias,
):
    requests = lax.axis_size("req")
    half = requests // 2
    own = jnp.transpose(transformer_tokens[0, :, 0, :])
    other = lax.ppermute(own, "req", [(i, (i + half) % requests) for i in range(requests)])
    shape = jax.ShapeDtypeStruct
    params = pltpu.CompilerParams(vmem_limit_bytes=60 * 1024 * 1024)
    pick, base, place = pl.pallas_call(
        plan_kernel,
        out_shape=(
            pltpu.VMEM((256, 128), BF16),
            pltpu.VMEM((128, 128), F32),
            pltpu.VMEM((448, 128), BF16),
        ),
        in_specs=[vmem_spec()] * 6,
        out_specs=(vmem_spec(),) * 3,
        scratch_shapes=[pltpu.VMEM((2, 256, 128), F32)],
        compiler_params=params,
    )(
        frames[None],
        heights[None],
        widths[None],
        jnp.transpose(tile_decode_device, (2, 1, 0)),
        jnp.transpose(tile_device_slot, (2, 1, 0)),
        own,
    )
    first = upsample_first_weight.reshape(27, CH, CH)
    sent = pl.pallas_call(
        pick_kernel,
        out_shape=pltpu.VMEM((SEQ, 8, 128), BF16),
        in_specs=[vmem_spec()] * 3,
        out_specs=vmem_spec(),
        compiler_params=pltpu.CompilerParams(vmem_limit_bytes=VMEM_LIMIT),
    )(held(other), held(pick), held(base))
    tokens = lax.all_to_all(sent, "seq", 0, 0, tiled=True)
    lanes, spread, stem, ready, biases = constants(
        sent, stem_conv_weight, first, (stem_conv_bias, upsample_first_bias, upsample_second_bias)
    )
    decoded = decode(
        held(tokens),
        held(place),
        held(lanes),
        held(spread),
        held(stem),
        held(ready),
        held(biases),
        first,
        upsample_second_weight,
    )
    return decoded.reshape(1, 1, 2, 2, 16, 16, CH)


def solution(mesh):
    placed = (P("req", None, "seq", None), P(), P(), P(), P(), P(), P(), P(), P(), P(), P(), P())
    return jax.shard_map(
        body,
        mesh=mesh,
        in_specs=placed,
        out_specs=P("req", "seq", None, None, None, None, None),
        check_vma=False,
    )
```
